32 devices in a mesh: dp: 8 (over z, core), pipe: 4 (over y, x).
Axes of the slice: x: 2, y: 2, z: 4, core: 2. Of those that a mesh axis runs over, the one named last changes fastest.
Arguments:
- acts_fwd: bfloat16 [4, 1024, 768], P('pipe', 'dp'), may hold values from -6 to 6
- acts_bwd: bfloat16 [4, 1024, 768], P('pipe', 'dp'), may hold values from -6 to 6
- cotangent: bfloat16 [4, 1024, 768], P('pipe', 'dp'), may hold values from -6 to 6
- lens_fwd: int32 [4, 8, 4], P('pipe', 'dp'), may hold values from 1 to 64, 128 in all within a row
- lens_bwd: int32 [4, 8, 4], P('pipe', 'dp'), may hold values from 1 to 64, 128 in all within a row
- w_proj: float32 [4, 768, 2048], P('pipe', 'dp'), may hold values from -0.21875 to 0.21875
- w_out: float32 [4, 512, 768], P('pipe', None, 'dp'), may hold values from -0.25 to 0.25
Outputs:
- next_acts: bfloat16 [4, 1024, 768], P('pipe', 'dp')
- prev_grads: bfloat16 [4, 1024, 768], P('pipe', 'dp')
- grad_proj: float32 [4, 768, 2048], P('pipe', 'dp')
- grad_out: float32 [4, 512, 768], P('pipe', None, 'dp')
The draws below stay inside these ranges and needn't reach their ends.
Inputs may be any that keep to these rules, and one draw needn't show every extreme that they name: `lens_fwd`: each row of 4 lengths sums to 128; its largest is exactly 64. `lens_bwd`: each row of 4 lengths sums to 128; its largest is exactly 64.
All inputs are finite; a program needn't handle non-finite values.
Results may differ from the reference program's by a relative error of at most 0.011.
Values may be sent and summed in bfloat16 or wider, within the bound.
A program may use at most 64 MiB of HBM per device.

```python
import math
import jax
import jax.numpy as jnp
import numpy as np
from jax import lax

D = 768
HEADS = 4
HEAD_DIM = 128
HID = 512
TOK_DEV = 128
USERS = 4
LMAX = 64
TOKENS = 1024
N_DP = 8
N_PIPE = 4


def with_spikes(array, key, source, target, blocks, factor):
    def block_of(position):
        return (jnp.arange(array.shape[position]) // (array.shape[position] // blocks)).reshape((-1,) + (1,) * (array.ndim - 1 - position))

    first = jax.random.permutation(key, blocks)[block_of(target)]
    far = (block_of(target) + blocks // 2) % blocks
    return jnp.where((block_of(source) == first) | (block_of(source) == far), factor * array, array)


def levels(key, shape, shards, smallest, top_value):
    factor_of = 1.0
    for dim, shards_of in shards:
        steps = jax.random.uniform(jax.random.fold_in(jax.random.fold_in(key, 6), dim), (shards_of,), jnp.float32, smallest / len(shards), top_value / len(shards))
        factor_of = factor_of * jnp.repeat(jnp.exp(steps), shape[dim] // shards_of).reshape((-1,) + (1,) * (len(shape) - 1 - dim))
    return factor_of


def profile(count, total, bound, slope):
    portions = [(1 << 20) // math.isqrt(standing ** slope) + 1 for standing in range(2, count + 1)]
    rest, counts = total - bound - (count - 1), [1] * (count - 1)
    while rest > 0:
        free = [i for i in range(count - 1) if counts[i] < bound]
        whole, budget = sum([portions[i] for i in free]), rest
        for i in free:
            more = min(bound - counts[i], max(1, budget * portions[i] // whole), rest)
            counts[i] = counts[i] + more
            rest = rest - more
    return np.array([bound] + counts)


def uneven_parts(rng, amount, total, limit, slope):
    if amount == 2:
        one = jax.random.randint(rng, (), max(1, total - limit), min(limit, total - 1) + 1)
        return jnp.stack([one, total - one])
    sizes = jnp.asarray(profile(amount, total, limit, slope), jnp.int32)
    twos = (amount - 1) // 2
    giver, taker = sizes[1:1 + 2 * twos:2], sizes[2:2 + 2 * twos:2]
    room = jnp.minimum(giver - 1, limit - taker)
    moved = jax.random.randint(jax.random.fold_in(rng, 1), (twos,), 0, 1 << 20) % (room + 1)
    sizes = sizes.at[1:1 + 2 * twos:2].set(giver - moved).at[2:2 + 2 * twos:2].set(taker + moved)
    return sizes[jax.random.permutation(jax.random.fold_in(rng, 2), amount)]


def noise(rng, shape, scale, most, cuts=(), held_as=jnp.bfloat16):
    values = jax.random.normal(rng, shape, jnp.float32) * scale
    if len(cuts) > 0:
        values = levels(rng, shape, cuts, -0.22, 0.18) * values
    return jnp.clip(values, min=-most, max=most).astype(held_as)


def bell_draw_with(rng, shape, spread, most, cuts, heavy, kind=jnp.bfloat16):
    array = spread * jax.random.normal(rng, shape, jnp.float32)
    if cuts:
        array = array * levels(rng, shape, cuts, -0.22, 0.18)
    return jnp.clip(with_spikes(array, jax.random.fold_in(rng, 3), *heavy), -most, most).astype(kind)


def setup_inputs(seed: int = 0) -> dict:
    key_list = jax.random.split(jax.random.key(seed), 8)
    acts_fwd = noise(key_list[0], (N_PIPE, TOKENS, D), 1.0, 6.0, ((0, 4), (1, 8)))
    acts_bwd = noise(key_list[1], (N_PIPE, TOKENS, D), 1.0, 6.0, ((0, 4), (1, 8)))
    cotangent = bell_draw_with(key_list[2], (N_PIPE, TOKENS, D), 1.0, 6.0, ((0, 4), (1, 8)), (1, 2, 8, 2.0))
    lens_fwd = jax.vmap(lambda own: uneven_parts(own, USERS, TOK_DEV, LMAX, 2))(jax.random.split(key_list[3], N_PIPE * N_DP)).reshape((N_PIPE, N_DP, USERS)).astype(jnp.int32)
    lens_bwd = jax.vmap(lambda own: uneven_parts(own, USERS, TOK_DEV, LMAX, 2))(jax.random.split(key_list[4], N_PIPE * N_DP)).reshape((N_PIPE, N_DP, USERS)).astype(jnp.int32)
    w_proj = noise(key_list[5], (N_PIPE, D, 4 * HID), D ** -0.5, 0.21875, ((0, 4), (1, 8)), jnp.float32)
    w_out = noise(key_list[6], (N_PIPE, HID, D), HID ** -0.5, 0.25, ((0, 4), (2, 8)), jnp.float32)
    return dict(acts_fwd=acts_fwd, acts_bwd=acts_bwd, cotangent=cotangent, lens_fwd=lens_fwd, lens_bwd=lens_bwd, w_proj=w_proj, w_out=w_out)


EPS = 1e-05

def jagged_mask(lengths, count):
    ends = jnp.cumsum(lengths).astype(jnp.int32)
    positions = jnp.arange(count, dtype=jnp.int32)
    segment = lax.optimization_barrier(jnp.sum((positions[:, None] >= ends[None, :]).astype(jnp.int32), axis=1))
    keep = (segment[:, None] == segment[None, :]) & (positions[:, None] >= positions[None, :])
    return keep.astype(jnp.float32)

def layer_norm(values):
    center = values - lax.optimization_barrier(jnp.mean(values, axis=-1, keepdims=True))
    inverse = lax.rsqrt(lax.optimization_barrier(jnp.mean(center * center, axis=-1, keepdims=True)) + EPS)
    return (center * inverse, inverse)

def norm_back(grad_normed, normed, inverse):
    return inverse * (grad_normed - lax.optimization_barrier(jnp.mean(grad_normed, axis=-1, keepdims=True)) - normed * lax.optimization_barrier(jnp.mean(grad_normed * normed, axis=-1, keepdims=True)))

def silu_slope(values):
    sigma = jax.nn.sigmoid(values)
    return sigma * (1.0 + values * (1.0 - sigma))

def forward_parts(tokens, w_first, keep):
    count = tokens.shape[0]
    tok_float = tokens.astype(jnp.float32)
    normed, inverse = layer_norm(tok_float)
    normed_bf = normed.astype(jnp.bfloat16)
    preact = jnp.dot(normed_bf, w_first, preferred_element_type=jnp.float32)
    hidden = jax.nn.silu(preact).astype(jnp.bfloat16)
    gate_u = hidden[:, :HID]
    values_h = hidden[:, HID:2 * HID].reshape(count, HEADS, HEAD_DIM)
    queries = hidden[:, 2 * HID:3 * HID].reshape(count, HEADS, HEAD_DIM)
    keys_h = hidden[:, 3 * HID:].reshape(count, HEADS, HEAD_DIM)
    scores = jnp.einsum('ihd,jhd->hij', queries.astype(jnp.float32), keys_h.astype(jnp.float32)) * HEAD_DIM ** (-0.5)
    attn = (jax.nn.silu(scores) * keep[None] * (1.0 / LMAX)).astype(jnp.bfloat16)
    mixed = jnp.einsum('hij,jhd->ihd', attn.astype(jnp.float32), values_h.astype(jnp.float32)).reshape(count, HID)
    mixed_n, inverse_o = layer_norm(mixed)
    gated = (mixed_n * gate_u.astype(jnp.float32)).astype(jnp.bfloat16)
    return (tok_float, normed, inverse, normed_bf, preact, gate_u, values_h, queries, keys_h, scores, attn, mixed_n, inverse_o, gated)

def forward(tokens, w_first, w_second, keep):
    parts = forward_parts(tokens, w_first, keep)
    return (parts[0] + jnp.dot(parts[13], w_second, preferred_element_type=jnp.float32)).astype(jnp.bfloat16)

def backward(tokens, cotan, w_first, w_second, keep):
    count = tokens.shape[0]
    tok_float, normed, inverse, normed_bf, preact, gate_u, values_h, queries, keys_h, scores, attn, mixed_n, inverse_o, gated = forward_parts(tokens, w_first, keep)
    grad_y = jnp.dot(cotan, w_second.T, preferred_element_type=jnp.float32)
    grad_u = grad_y * mixed_n
    grad_mn = grad_y * gate_u.astype(jnp.float32)
    grad_mixed = norm_back(grad_mn, mixed_n, inverse_o).astype(jnp.bfloat16).reshape(count, HEADS, HEAD_DIM)
    grad_attn = jnp.einsum('ihd,jhd->hij', grad_mixed.astype(jnp.float32), values_h.astype(jnp.float32))
    grad_vals = jnp.einsum('hij,ihd->jhd', attn.astype(jnp.float32), grad_mixed.astype(jnp.float32))
    grad_scores = (grad_attn * keep[None] * (1.0 / LMAX) * silu_slope(scores) * HEAD_DIM ** (-0.5)).astype(jnp.bfloat16)
    grad_q = jnp.einsum('hij,jhd->ihd', grad_scores.astype(jnp.float32), keys_h.astype(jnp.float32))
    grad_k = jnp.einsum('hij,ihd->jhd', grad_scores.astype(jnp.float32), queries.astype(jnp.float32))
    grad_hidden = jnp.concatenate([grad_u, grad_vals.reshape(count, HID), grad_q.reshape(count, HID), grad_k.reshape(count, HID)], axis=1)
    grad_pre = (grad_hidden * silu_slope(preact)).astype(jnp.bfloat16)
    grad_norm = jnp.dot(grad_pre, w_first.T, preferred_element_type=jnp.float32)
    grad_in = (cotan.astype(jnp.float32) + norm_back(grad_norm, normed, inverse)).astype(jnp.bfloat16)
    return (grad_in, normed_bf, grad_pre, gated)

def reference(acts_fwd, acts_bwd, cotangent, lens_fwd, lens_bwd, w_proj, w_out):
    loss_scale = 1.0 / math.sqrt(N_DP * TOK_DEV)

    def phase(items):
        fwd_rows, bwd_rows, cot_rows, fwd_lens, bwd_lens, proj_master, out_master = items
        w_first = proj_master.astype(jnp.bfloat16)
        w_second = out_master.astype(jnp.bfloat16)

        def block(carry, entry):
            fwd_x, bwd_x, cotan, fwd_len, bwd_len = entry
            result = forward(fwd_x, w_first, w_second, jagged_mask(fwd_len, TOK_DEV))
            grad_in, normed_bf, grad_pre, gated = backward(bwd_x, cotan, w_first, w_second, jagged_mask(bwd_len, TOK_DEV))
            term_proj = jnp.dot(normed_bf.T, grad_pre, preferred_element_type=jnp.float32) * loss_scale
            term_out = jnp.dot(gated.T, cotan, preferred_element_type=jnp.float32) * loss_scale
            return ((carry[0] + term_proj, carry[1] + term_out), (result, grad_in))
        start = (jnp.zeros((D, 4 * HID), jnp.float32), jnp.zeros((HID, D), jnp.float32))
        entries = (fwd_rows.reshape(N_DP, TOK_DEV, D), bwd_rows.reshape(N_DP, TOK_DEV, D), cot_rows.reshape(N_DP, TOK_DEV, D), fwd_lens, bwd_lens)
        sums, stacked = lax.scan(block, start, entries)
        return (stacked[0].reshape(TOKENS, D), stacked[1].reshape(TOKENS, D), sums[0], sums[1])
    outputs, grads_in, grad_proj, grad_out = lax.map(phase, (acts_fwd, acts_bwd, cotangent, lens_fwd, lens_bwd, w_proj, w_out))
    next_acts = jnp.roll(outputs, 1, axis=0)
    prev_grads = jnp.roll(grads_in, -1, axis=0)
    return (next_acts, prev_grads, grad_proj, grad_out)
```

```python
import functools
import math

import jax
import jax.numpy as jnp
from jax import lax
from jax.experimental import pallas as pl
from jax.experimental.pallas import tpu as pltpu
from jax.sharding import PartitionSpec as P

HEADS = 4
HEAD_DIM = 128
LMAX = 64
EPS = 1e-05
CORES = 2
MESH = pl.DeviceIdType.MESH
BF = jnp.bfloat16
F32 = jnp.float32

NN = (((1,), (0,)), ((), ()))
NT = (((1,), (1,)), ((), ()))
TN = (((0,), (0,)), ((), ()))


def dot(a, b, dims=NN):
    return lax.dot_general(a, b, dims, preferred_element_type=F32)


def sigmoid(v):
    return 0.5 + 0.5 * jnp.tanh(0.5 * v)


def layer_norm(values):
    center = values - jnp.mean(values, axis=-1, keepdims=True)
    inverse = lax.rsqrt(jnp.mean(center * center, axis=-1, keepdims=True) + EPS)
    return center * inverse, inverse


def norm_back(grad, normed, inverse):
    return inverse * (
        grad
        - jnp.mean(grad, axis=-1, keepdims=True)
        - normed * jnp.mean(grad * normed, axis=-1, keepdims=True)
    )


def jagged_mask(lens_ref, count):
    rows = lax.broadcasted_iota(jnp.int32, (count, count), 0)
    cols = lax.broadcasted_iota(jnp.int32, (count, count), 1)
    row_seg = jnp.zeros((count, count), jnp.int32)
    col_seg = jnp.zeros((count, count), jnp.int32)
    end = jnp.int32(0)
    for user in range(lens_ref.shape[2]):
        end = end + lens_ref[0, 0, user]
        row_seg += jnp.where(rows >= end, 1, 0)
        col_seg += jnp.where(cols >= end, 1, 0)
    keep = (row_seg == col_seg) & (cols <= rows)
    return jnp.where(keep, 1.0 / LMAX, 0.0)


def kernel(
    chips,
    phases,
    xf_ref,
    xb_ref,
    g_ref,
    lf_ref,
    lb_ref,
    w_ref,
    next_ref,
    prev_ref,
    gp_ref,
    go_ref,
    wall,
    xnf,
    xnb,
    normed_ref,
    norm_t,
    g_t,
    hidden,
    slope,
    gpre,
    gated_b,
    gnorm,
    fwd_out,
    bwd_out,
    own,
    psend,
    precv,
    lrecv,
    rrecv,
    stage,
    ag_right,
    ag_left,
    ag_part,
    ag_chain,
    ag_precv,
    rs_send,
    rs_part,
    rs_precv,
    rs_lrecv,
    rs_rrecv,
    pipe_sems,
):
    shard, wide = w_ref.shape
    count, model = xf_ref.shape[1:]
    hid = HEADS * HEAD_DIM
    proj = 4 * hid
    scale = HEAD_DIM ** (-0.5)
    loss_scale = 1.0 / math.sqrt(chips * CORES * count)
    me = lax.axis_index("dp")
    phase = lax.axis_index("pipe")
    z, c = lax.div(me, CORES), lax.rem(me, CORES)
    has_left, has_right = z > 0, z < chips - 1
    left, right, partner = {"dp": me - CORES}, {"dp": me + CORES}, {"dp": z * CORES + 1 - c}
    ahead = {"pipe": lax.rem(phase + 1, phases)}
    behind = {"pipe": lax.rem(phase + phases - 1, phases)}

    barrier = pltpu.get_barrier_semaphore()

    def greet(target):
        pl.semaphore_signal(barrier, inc=1, device_id=target, device_id_type=MESH)

    @pl.when(has_left)
    def _():
        greet(left)

    @pl.when(has_right)
    def _():
        greet(right)

    greet(partner)
    greet(ahead)
    greet(behind)

    def rows(chip, core):
        return pl.ds(pl.multiple_of((chip * CORES + core) * shard, shard), shard)

    wall[rows(z, c), :] = w_ref[...]

    neighbours = 3 + jnp.where(has_left, 1, 0) + jnp.where(has_right, 1, 0)
    pl.semaphore_wait(barrier, neighbours)

    def remote(src, dst, send_sem, recv_sem, target):
        return pltpu.make_async_remote_copy(
            src_ref=src,
            dst_ref=dst,
            send_sem=send_sem,
            recv_sem=recv_sem,
            device_id=target,
            device_id_type=MESH,
        )

    def gather(chip, core, send_sem, recv_sem, target):
        block = wall.at[rows(chip, core), :]
        return remote(block, block, send_sem.at[chip], recv_sem.at[chip], target)

    def to_right(chip):
        return gather(chip, c, ag_right, ag_chain, right)

    def to_left(chip):
        return gather(chip, c, ag_left, ag_chain, left)

    def to_partner(chip):
        return gather(chip, c, ag_part, ag_precv, partner)

    def from_partner(chip):
        return gather(chip, 1 - c, ag_part, ag_precv, partner)

    @pl.when(has_right)
    def _():
        to_right(z).start()

    @pl.when(has_left)
    def _():
        to_left(z).start()

    to_partner(z).start()

    normed_f, _ = layer_norm(xf_ref[0].astype(F32))
    xnf[...] = normed_f.astype(BF)
    normed_b, inverse_b = layer_norm(xb_ref[0].astype(F32))
    normed_ref[...] = normed_b
    xnb[...] = normed_b.astype(BF)
    norm_t[...] = normed_b.T.astype(BF)
    g_t[...] = g_ref[0].astype(F32).T.astype(BF)
    keep_b = jagged_mask(lb_ref, count)

    def gather_tick(t, carry):
        from_left, from_right = z - t, z + t

        @pl.when(from_left >= 0)
        def _():
            to_right(from_left).wait_recv()

            @pl.when(has_right)
            def _():
                to_right(from_left).start()

            to_partner(from_left).start()

        @pl.when(from_right < chips)
        def _():
            to_left(from_right).wait_recv()

            @pl.when(has_left)
            def _():
                to_left(from_right).start()

            to_partner(from_right).start()

        return carry

    lax.fori_loop(1, chips, gather_tick, 0)

    def partner_arrival(j, carry):
        from_partner(j).wait_recv()
        return carry

    lax.fori_loop(0, chips, partner_arrival, 0)

    tile = 256

    def project(x_ref, with_slope):
        def body(i, carry):
            cols = pl.ds(pl.multiple_of(i * tile, tile), tile)
            value = dot(x_ref[...], wall[:, cols])
            sigma = sigmoid(value)
            silu = value * sigma
            hidden[:, cols] = silu.astype(BF)
            if with_slope:
                slope[:, cols] = sigma + silu * (1.0 - sigma)
            return carry

        lax.fori_loop(0, proj // tile, body, 0)

    def part(which, head):
        start = which * hid + head * HEAD_DIM
        return hidden[:, start : start + HEAD_DIM]

    def attend(keep):
        sigmas, scores, attns, mixed = [], [], [], []
        for head in range(HEADS):
            score = dot(part(2, head), part(3, head), NT) * scale
            sigma = sigmoid(score)
            attn = (score * sigma * keep).astype(BF)
            mixed.append(dot(attn, part(1, head)))
            scores.append(score)
            sigmas.append(sigma)
            attns.append(attn)
        return sigmas, scores, attns, jnp.concatenate(mixed, axis=1)

    project(xnb, True)
    sigmas, scores, attns, mixed = attend(keep_b)
    mixed_n, inverse_o = layer_norm(mixed)
    gate = hidden[:, :hid].astype(F32)
    gated_b[...] = (mixed_n * gate).astype(BF)
    grad_y = dot(g_ref[0], wall[:, proj:])
    gpre[:, :hid] = (grad_y * mixed_n * slope[:, :hid]).astype(BF)
    grad_mixed = norm_back(grad_y * gate, mixed_n, inverse_o).astype(BF)
    for head in range(HEADS):
        grad_m = grad_mixed[:, head * HEAD_DIM : (head + 1) * HEAD_DIM]
        score, sigma = scores[head], sigmas[head]
        grad_attn = dot(grad_m, part(1, head), NT)
        grad_vals = dot(attns[head], grad_m, TN)
        grad_s = (
            grad_attn * keep_b * (sigma * (1.0 + score * (1.0 - sigma))) * scale
        ).astype(BF)
        grad_q = dot(grad_s, part(3, head))
        grad_k = dot(grad_s, part(2, head), TN)
        for which, grad in ((1, grad_vals), (2, grad_q), (3, grad_k)):
            start = which * hid + head * HEAD_DIM
            cols = slice(start, start + HEAD_DIM)
            gpre[:, cols] = (grad * slope[:, cols]).astype(BF)

    def part_copy(d):
        return remote(psend.at[d], precv.at[d], rs_part.at[d], rs_precv.at[d], partner)

    def right_copy(d):
        return remote(stage.at[d], lrecv.at[d], rs_send.at[d], rs_lrecv.at[d], right)

    def left_copy(d):
        return remote(stage.at[d], rrecv.at[d], rs_send.at[d], rs_rrecv.at[d], left)

    def term(k, carry):
        d = jnp.where(z < chips // 2, chips - 1 - k, k)
        other = rows(d, 1 - c)
        psend[d, :, :proj] = (dot(norm_t[other, :], gpre[...]) * loss_scale).astype(BF)
        psend[d, :, proj:] = (dot(g_t[other, :], gated_b[...]) * loss_scale).astype(BF)
        part_copy(d).start()
        mine = rows(d, c)
        own[d, :, :proj] = dot(norm_t[mine, :], gpre[...]) * loss_scale
        own[d, :, proj:] = dot(g_t[mine, :], gated_b[...]) * loss_scale
        return carry

    def chip_sum(d):
        part_copy(d).wait_recv()
        return own[d] + precv[d].astype(F32)

    def reduce_tick(tau, carry):
        @pl.when(has_right & (tau >= z))
        def _():
            d = chips - 1 - tau + z
            own[d] = chip_sum(d)

            @pl.when(has_left)
            def _():
                right_copy(d).wait_recv()
                own[d] = own[d] + lrecv[d].astype(F32)

            stage[d] = own[d].astype(BF)
            right_copy(d).start()

        @pl.when(has_left & (tau >= chips - 1 - z))
        def _():
            d = tau - (chips - 1 - z)
            own[d] = chip_sum(d)

            @pl.when(has_right)
            def _():
                left_copy(d).wait_recv()
                own[d] = own[d] + rrecv[d].astype(F32)

            stage[d] = own[d].astype(BF)
            left_copy(d).start()

        return carry

    early = min(2, chips)
    lax.fori_loop(0, early, term, 0)
    lax.fori_loop(0, 1, reduce_tick, 0)
    lax.fori_loop(early, chips, term, 0)

    row_tile = 256

    def norm_grad(i, carry):
        at = pl.ds(pl.multiple_of(i * row_tile, row_tile), row_tile)
        gnorm[:, at] = dot(gpre[...], wall[at, :proj], NT)
        return carry

    lax.fori_loop(0, model // row_tile, norm_grad, 0)
    grad_in = g_ref[0].astype(F32) + norm_back(gnorm[...], normed_ref[...], inverse_b)
    bwd_out[...] = grad_in.astype(BF)
    send_bwd = remote(bwd_out, prev_ref.at[0], pipe_sems.at[0], pipe_sems.at[1], behind)
    send_bwd.start()

    project(xnf, False)
    _, _, _, mixed_f = attend(jagged_mask(lf_ref, count))
    gated_f = (layer_norm(mixed_f)[0] * hidden[:, :hid].astype(F32)).astype(BF)
    result = xf_ref[0].astype(F32) + dot(gated_f, wall[:, proj:], NT)
    fwd_out[...] = result.astype(BF)
    send_fwd = remote(fwd_out, next_ref.at[0], pipe_sems.at[2], pipe_sems.at[3], ahead)
    send_fwd.start()

    lax.fori_loop(1, chips - 1, reduce_tick, 0)
    own[z] = chip_sum(z)

    @pl.when(has_left)
    def _():
        right_copy(z).wait_recv()
        own[z] = own[z] + lrecv[z].astype(F32)

    @pl.when(has_right)
    def _():
        left_copy(z).wait_recv()
        own[z] = own[z] + rrecv[z].astype(F32)

    gp_ref[0] = own[z, :, :proj]
    go_ref[...] = own[z, :, proj:]

    send_bwd.wait()
    send_fwd.wait()

    def drain(j, carry):
        to_partner(j).wait_send()
        part_copy(j).wait_send()

        @pl.when(has_right & (j <= z))
        def _():
            to_right(j).wait_send()

        @pl.when(has_left & (j >= z))
        def _():
            to_left(j).wait_send()

        @pl.when(j != z)
        def _():
            right_copy(j).wait_send()

        return carry

    lax.fori_loop(0, chips, drain, 0)


def per_device(acts_fwd, acts_bwd, cotangent, lens_fwd, lens_bwd, w_proj, w_out):
    chips = lax.axis_size("dp") // CORES
    phases = lax.axis_size("pipe")
    _, count, model = acts_fwd.shape
    _, shard, proj = w_proj.shape
    hid = w_out.shape[1]
    wide = proj + hid
    weights = jnp.concatenate([w_proj[0], w_out[0].T], axis=1).astype(BF)
    vmem = pl.BlockSpec(memory_space=pltpu.VMEM)
    smem = pl.BlockSpec(memory_space=pltpu.SMEM)
    dma = pltpu.SemaphoreType.DMA
    flops = 2 * count * model * (2 * proj + 2 * proj + 4 * hid)
    next_acts, prev_grads, grad_proj, grad_out = pl.pallas_call(
        functools.partial(kernel, chips, phases),
        out_shape=(
            jax.ShapeDtypeStruct((1, count, model), BF),
            jax.ShapeDtypeStruct((1, count, model), BF),
            jax.ShapeDtypeStruct((1, shard, proj), F32),
            jax.ShapeDtypeStruct((shard, hid), F32),
        ),
        in_specs=[vmem, vmem, vmem, smem, smem, vmem],
        out_specs=(vmem, vmem, vmem, vmem),
        scratch_shapes=[
            pltpu.VMEM((model, wide), BF),
            pltpu.VMEM((count, model), BF),
            pltpu.VMEM((count, model), BF),
            pltpu.VMEM((count, model), F32),
            pltpu.VMEM((model, count), BF),
            pltpu.VMEM((model, count), BF),
            pltpu.VMEM((count, proj), BF),
            pltpu.VMEM((count, proj), F32),
            pltpu.VMEM((count, proj), BF),
            pltpu.VMEM((count, hid), BF),
            pltpu.VMEM((count, model), F32),
            pltpu.VMEM((count, model), BF),
            pltpu.VMEM((count, model), BF),
            pltpu.VMEM((chips, shard, wide), F32),
            pltpu.VMEM((chips, shard, wide), BF),
            pltpu.VMEM((chips, shard, wide), BF),
            pltpu.VMEM((chips, shard, wide), BF),
            pltpu.VMEM((chips, shard, wide), BF),
            pltpu.VMEM((chips, shard, wide), BF),
        ]
        + [dma((chips,))] * 10
        + [dma((4,))],
        compiler_params=pltpu.CompilerParams(
            collective_id=0, has_side_effects=True, vmem_limit_bytes=56 * 1024 * 1024
        ),
        cost_estimate=pl.CostEstimate(
            flops=flops, bytes_accessed=4 * model * wide, transcendentals=2 * count * proj
        ),
    )(acts_fwd, acts_bwd, cotangent, lens_fwd, lens_bwd, weights)
    return next_acts, prev_grads, grad_proj, grad_out.T[None]


def solution(mesh):
    return jax.shard_map(
        per_device,
        mesh=mesh,
        in_specs=(
            P("pipe", "dp", None),
            P("pipe", "dp", None),
            P("pipe", "dp", None),
            P("pipe", "dp", None),
            P("pipe", "dp", None),
            P("pipe", "dp", None),
            P("pipe", None, "dp"),
        ),
        out_specs=(
            P("pipe", "dp", None),
            P("pipe", "dp", None),
            P("pipe", "dp", None),
            P("pipe", None, "dp"),
        ),
        check_vma=False,
    )
```

```python
import functools
import math

import jax
import jax.numpy as jnp
from jax import lax
from jax.experimental import pallas as pl
from jax.experimental.pallas import tpu as pltpu
from jax.sharding import PartitionSpec as P

HEADS = 4
HEAD_DIM = 128
LMAX = 64
EPS = 1e-05
CORES = 2
PARTS = 5
MESH = pl.DeviceIdType.MESH
BF = jnp.bfloat16
F32 = jnp.float32

NN = (((1,), (0,)), ((), ()))
NT = (((1,), (1,)), ((), ()))
TN = (((0,), (0,)), ((), ()))


def dot(a, b, dims=NN):
    return lax.dot_general(a, b, dims, preferred_element_type=F32)


def sigmoid(v):
    return 0.5 + 0.5 * jnp.tanh(0.5 * v)


def layer_norm(values):
    center = values - jnp.mean(values, axis=-1, keepdims=True)
    inverse = lax.rsqrt(jnp.mean(center * center, axis=-1, keepdims=True) + EPS)
    return center * inverse, inverse


def norm_back(grad, normed, inverse):
    return inverse * (
        grad
        - jnp.mean(grad, axis=-1, keepdims=True)
        - normed * jnp.mean(grad * normed, axis=-1, keepdims=True)
    )


def jagged_mask(lens_ref, count):
    rows = lax.broadcasted_iota(jnp.int32, (count, count), 0)
    cols = lax.broadcasted_iota(jnp.int32, (count, count), 1)
    row_seg = jnp.zeros((count, count), jnp.int32)
    col_seg = jnp.zeros((count, count), jnp.int32)
    end = jnp.int32(0)
    for user in range(lens_ref.shape[2]):
        end = end + lens_ref[0, 0, user]
        row_seg += jnp.where(rows >= end, 1, 0)
        col_seg += jnp.where(cols >= end, 1, 0)
    keep = (row_seg == col_seg) & (cols <= rows)
    return jnp.where(keep, 1.0 / LMAX, 0.0)


def kernel(
    chips,
    phases,
    xf_ref,
    xb_ref,
    g_ref,
    lf_ref,
    lb_ref,
    wp_ref,
    wo_ref,
    next_ref,
    prev_ref,
    gp_ref,
    go_ref,
    wall,
    xnf,
    xnb,
    normed_ref,
    norm_t,
    g_t,
    hidden,
    slope,
    gpre,
    gated_b,
    gnorm,
    fwd_out,
    bwd_out,
    own,
    psend,
    precv,
    lrecv,
    rrecv,
    stage,
    ag_right,
    ag_left,
    ag_part,
    ag_chain,
    ag_precv,
    rs_send,
    rs_part,
    rs_precv,
    rs_lrecv,
    rs_rrecv,
    pipe_sems,
):
    val, que, key, gat, out = range(PARTS)
    shard, hid = wo_ref.shape
    count, model = xf_ref.shape[1:]
    scale = HEAD_DIM ** (-0.5)
    loss_scale = 1.0 / math.sqrt(chips * CORES * count)
    me = lax.axis_index("dp")
    phase = lax.axis_index("pipe")
    z, c = lax.div(me, CORES), lax.rem(me, CORES)
    has_left, has_right = z > 0, z < chips - 1
    middle = has_left & has_right
    end = jnp.logical_not(middle)
    left, right, partner = {"dp": me - CORES}, {"dp": me + CORES}, {"dp": z * CORES + 1 - c}
    ahead = {"pipe": lax.rem(phase + 1, phases)}
    behind = {"pipe": lax.rem(phase + phases - 1, phases)}

    barrier = pltpu.get_barrier_semaphore()

    def greet(target):
        pl.semaphore_signal(barrier, inc=1, device_id=target, device_id_type=MESH)

    @pl.when(has_left)
    def _():
        greet(left)

    @pl.when(has_right)
    def _():
        greet(right)

    greet(partner)
    greet(ahead)
    greet(behind)

    def rows(chip, core):
        return pl.ds(pl.multiple_of((chip * CORES + core) * shard, shard), shard)

    def home(i):
        start = (i + 1) % (PARTS - 1) * hid
        return slice(start, start + hid)

    for i in (val, que, key, gat):
        wall[i, rows(z, c), :] = wp_ref[0, :, home(i)].astype(BF)
    wall[out, rows(z, c), :] = wo_ref[...].astype(BF)

    neighbours = 3 + jnp.where(has_left, 1, 0) + jnp.where(has_right, 1, 0)
    pl.semaphore_wait(barrier, neighbours)

    def remote(src, dst, send_sem, recv_sem, target):
        return pltpu.make_async_remote_copy(
            src_ref=src,
            dst_ref=dst,
            send_sem=send_sem,
            recv_sem=recv_sem,
            device_id=target,
            device_id_type=MESH,
        )

    def gather(i, chip, core, send_sem, recv_sem, target):
        block = wall.at[i, rows(chip, core), :]
        return remote(block, block, send_sem.at[i, chip], recv_sem.at[i, chip], target)

    def to_right(i, chip):
        return gather(i, chip, c, ag_right, ag_chain, right)

    def to_left(i, chip):
        return gather(i, chip, c, ag_left, ag_chain, left)

    def to_partner(i, chip):
        return gather(i, chip, c, ag_part, ag_precv, partner)

    def from_partner(i, chip):
        return gather(i, chip, 1 - c, ag_part, ag_precv, partner)

    def start_own(i):
        @pl.when(has_right)
        def _():
            to_right(i, z).start()

        @pl.when(has_left)
        def _():
            to_left(i, z).start()

        to_partner(i, z).start()

    def loop(lower, upper, body):
        def step(i, carry):
            body(i)
            return carry

        lax.fori_loop(lower, upper, step, 0)

    ahead_parts = 2
    loop(0, ahead_parts, start_own)

    @pl.when(end)
    def _():
        loop(ahead_parts, PARTS, start_own)

    normed_b, inverse_b = layer_norm(xb_ref[0].astype(F32))
    normed_ref[...] = normed_b
    xnb[...] = normed_b.astype(BF)
    normed_f, _ = layer_norm(xf_ref[0].astype(F32))
    xnf[...] = normed_f.astype(BF)
    norm_t[...] = normed_b.T.astype(BF)
    g_t[...] = g_ref[0].astype(F32).T.astype(BF)
    keep_b = jagged_mask(lb_ref, count)

    def relay(i):
        def tick(t):
            from_left, from_right = z - t, z + t

            @pl.when(from_left >= 0)
            def _():
                to_right(i, from_left).wait_recv()

                @pl.when(has_right)
                def _():
                    to_right(i, from_left).start()

                to_partner(i, from_left).start()

            @pl.when(from_right < chips)
            def _():
                to_left(i, from_right).wait_recv()

                @pl.when(has_left)
                def _():
                    to_left(i, from_right).start()

                to_partner(i, from_right).start()

        loop(1, chips, tick)

    def arrivals(i):
        loop(0, chips, lambda j: from_partner(i, j).wait_recv())

    def project(x_ref, i, with_slope):
        value = dot(x_ref[...], wall[i])
        sigma = sigmoid(value)
        silu = value * sigma
        hidden[i] = silu.astype(BF)
        if with_slope:
            slope[i] = sigma + silu * (1.0 - sigma)

    def part(i, head):
        return hidden[i, :, head * HEAD_DIM : (head + 1) * HEAD_DIM]

    def attend(keep):
        sigmas, scores, attns, mixed = [], [], [], []
        for head in range(HEADS):
            score = dot(part(que, head), part(key, head), NT) * scale
            sigma = sigmoid(score)
            attn = (score * sigma * keep).astype(BF)
            mixed.append(dot(attn, part(val, head)))
            scores.append(score)
            sigmas.append(sigma)
            attns.append(attn)
        return sigmas, scores, attns, jnp.concatenate(mixed, axis=1)

    def send_forward():
        return remote(fwd_out, next_ref.at[0], pipe_sems.at[2], pipe_sems.at[3], ahead)

    def send_backward():
        return remote(bwd_out, prev_ref.at[0], pipe_sems.at[0], pipe_sems.at[1], behind)

    def forward_block():
        loop(0, PARTS - 1, lambda i: project(xnf, i, False))
        _, _, _, mixed_f = attend(jagged_mask(lf_ref, count))
        gated_f = (layer_norm(mixed_f)[0] * hidden[gat].astype(F32)).astype(BF)
        result = xf_ref[0].astype(F32) + dot(gated_f, wall[out], NT)
        fwd_out[...] = result.astype(BF)
        send_forward().start()

    def part_copy(i, d):
        return remote(psend.at[i, d], precv.at[i, d], rs_part.at[i, d], rs_precv.at[i, d], partner)

    def right_copy(i, d):
        return remote(stage.at[i, d], lrecv.at[i, d], rs_send.at[i, d], rs_lrecv.at[i, d], right)

    def left_copy(i, d):
        return remote(stage.at[i, d], rrecv.at[i, d], rs_send.at[i, d], rs_rrecv.at[i, d], left)

    def terms(i):
        sides, factor = (g_t, gated_b[...]) if i == out else (norm_t, gpre[i])

        def term(k):
            d = jnp.where(z < chips // 2, chips - 1 - k, k)
            psend[i, d] = (dot(sides[rows(d, 1 - c), :], factor) * loss_scale).astype(BF)
            part_copy(i, d).start()
            own[i, d] = dot(sides[rows(d, c), :], factor) * loss_scale

        loop(0, chips, term)

    def chip_sum(i, d):
        part_copy(i, d).wait_recv()
        return own[i, d] + precv[i, d].astype(F32)

    def reduce(i):
        def tick(tau):
            @pl.when(has_right & (tau >= z))
            def _():
                d = chips - 1 - tau + z
                own[i, d] = chip_sum(i, d)

                @pl.when(has_left)
                def _():
                    right_copy(i, d).wait_recv()
                    own[i, d] = own[i, d] + lrecv[i, d].astype(F32)

                stage[i, d] = own[i, d].astype(BF)
                right_copy(i, d).start()

            @pl.when(has_left & (tau >= chips - 1 - z))
            def _():
                d = tau - (chips - 1 - z)
                own[i, d] = chip_sum(i, d)

                @pl.when(has_right)
                def _():
                    left_copy(i, d).wait_recv()
                    own[i, d] = own[i, d] + rrecv[i, d].astype(F32)

                stage[i, d] = own[i, d].astype(BF)
                left_copy(i, d).start()

        loop(0, chips - 1, tick)

    @pl.when(middle)
    def _():
        def pass_on(i):
            relay(i)

            @pl.when(i + ahead_parts < PARTS)
            def _():
                start_own(i + ahead_parts)

        loop(0, PARTS, pass_on)
        loop(0, PARTS, arrivals)
        forward_block()

    @pl.when(end)
    def _():
        loop(0, gat, relay)
        loop(0, gat, arrivals)

    loop(0, gat, lambda i: project(xnb, i, True))
    sigmas, scores, attns, mixed = attend(keep_b)
    mixed_n, inverse_o = layer_norm(mixed)

    @pl.when(end)
    def _():
        relay(gat)
        arrivals(gat)

    project(xnb, gat, True)
    gate = hidden[gat].astype(F32)
    gated_b[...] = (mixed_n * gate).astype(BF)
    terms(out)

    @pl.when(end)
    def _():
        reduce(out)
        relay(out)
        arrivals(out)

    grad_y = dot(g_ref[0], wall[out])
    gpre[gat] = (grad_y * mixed_n * slope[gat]).astype(BF)
    terms(gat)
    grad_mixed = norm_back(grad_y * gate, mixed_n, inverse_o).astype(BF)
    heads = [slice(head * HEAD_DIM, (head + 1) * HEAD_DIM) for head in range(HEADS)]
    for head, cols in enumerate(heads):
        grad_vals = dot(attns[head], grad_mixed[:, cols], TN)
        gpre[val, :, cols] = (grad_vals * slope[val, :, cols]).astype(BF)
    terms(val)

    @pl.when(end)
    def _():
        reduce(gat)

    for head, cols in enumerate(heads):
        score, sigma = scores[head], sigmas[head]
        grad_attn = dot(grad_mixed[:, cols], part(val, head), NT)
        grad_s = (
            grad_attn * keep_b * (sigma * (1.0 + score * (1.0 - sigma))) * scale
        ).astype(BF)
        grad_q = dot(grad_s, part(key, head))
        grad_k = dot(grad_s, part(que, head), TN)
        gpre[que, :, cols] = (grad_q * slope[que, :, cols]).astype(BF)
        gpre[key, :, cols] = (grad_k * slope[key, :, cols]).astype(BF)
    terms(que)

    @pl.when(end)
    def _():
        reduce(val)

    terms(key)

    @pl.when(end)
    def _():
        reduce(que)
        reduce(key)

    @pl.when(middle)
    def _():
        reduce(out)
        reduce(gat)

    row_tile = 256

    def norm_grad(n):
        at = pl.ds(pl.multiple_of(n * row_tile, row_tile), row_tile)
        total = dot(gpre[val], wall[val, at, :], NT)
        for i in (que, key, gat):
            total += dot(gpre[i], wall[i, at, :], NT)
        gnorm[:, at] = total

    loop(0, model // row_tile, norm_grad)
    grad_in = g_ref[0].astype(F32) + norm_back(gnorm[...], normed_ref[...], inverse_b)
    bwd_out[...] = grad_in.astype(BF)
    send_backward().start()

    @pl.when(middle)
    def _():
        reduce(val)
        reduce(que)
        reduce(key)

    @pl.when(end)
    def _():
        forward_block()

    for i in (out, gat, val, que, key):
        own[i, z] = chip_sum(i, z)

        @pl.when(has_left)
        def _():
            right_copy(i, z).wait_recv()
            own[i, z] = own[i, z] + lrecv[i, z].astype(F32)

        @pl.when(has_right)
        def _():
            left_copy(i, z).wait_recv()
            own[i, z] = own[i, z] + rrecv[i, z].astype(F32)

        if i == out:
            go_ref[...] = own[i, z]
        else:
            gp_ref[0, :, home(i)] = own[i, z]

    send_backward().wait()
    send_forward().wait()

    def drain(j):
        def each(i):
            to_partner(i, j).wait_send()
            part_copy(i, j).wait_send()

            @pl.when(has_right & (j <= z))
            def _():
                to_right(i, j).wait_send()

            @pl.when(has_left & (j >= z))
            def _():
                to_left(i, j).wait_send()

            @pl.when(j != z)
            def _():
                right_copy(i, j).wait_send()

        loop(0, PARTS, each)

    loop(0, chips, drain)


def finish(*refs):
    sems = refs[-1]
    half = (len(refs) - 1) // 2
    copies = [
        pltpu.make_async_copy(src, dst, sems.at[n])
        for n, (src, dst) in enumerate(zip(refs[:half], refs[half:-1]))
    ]
    for copy in copies:
        copy.start()
    for copy in copies:
        copy.wait()


def per_device(acts_fwd, acts_bwd, cotangent, lens_fwd, lens_bwd, w_proj, w_out):
    chips = lax.axis_size("dp") // CORES
    phases = lax.axis_size("pipe")
    _, count, model = acts_fwd.shape
    _, shard, proj = w_proj.shape
    hid = w_out.shape[1]
    vmem = pl.BlockSpec(memory_space=pltpu.VMEM)
    smem = pl.BlockSpec(memory_space=pltpu.SMEM)
    hbm = pl.BlockSpec(memory_space=pl.ANY)
    dma = pltpu.SemaphoreType.DMA
    slots = pltpu.VMEM((PARTS, chips, shard, hid), BF)
    flops = 2 * count * model * (2 * proj + 2 * proj + 4 * hid)
    results = (
        jax.ShapeDtypeStruct((1, count, model), BF),
        jax.ShapeDtypeStruct((1, count, model), BF),
        jax.ShapeDtypeStruct((1, shard, proj), F32),
        jax.ShapeDtypeStruct((shard, hid), F32),
    )
    outs = pl.pallas_call(
        functools.partial(kernel, chips, phases),
        out_shape=results,
        in_specs=[vmem, vmem, vmem, smem, smem, vmem, vmem],
        out_specs=(vmem, vmem, vmem, vmem),
        scratch_shapes=[
            pltpu.VMEM((PARTS, model, hid), BF),
            pltpu.VMEM((count, model), BF),
            pltpu.VMEM((count, model), BF),
            pltpu.VMEM((count, model), F32),
            pltpu.VMEM((model, count), BF),
            pltpu.VMEM((model, count), BF),
            pltpu.VMEM((PARTS - 1, count, hid), BF),
            pltpu.VMEM((PARTS - 1, count, hid), F32),
            pltpu.VMEM((PARTS - 1, count, hid), BF),
            pltpu.VMEM((count, hid), BF),
            pltpu.VMEM((count, model), F32),
            pltpu.VMEM((count, model), BF),
            pltpu.VMEM((count, model), BF),
            pltpu.VMEM((PARTS, chips, shard, hid), F32),
            slots,
            slots,
            slots,
            slots,
            slots,
        ]
        + [dma((PARTS, chips))] * 10
        + [dma((4,))],
        compiler_params=pltpu.CompilerParams(
            collective_id=0, has_side_effects=True, vmem_limit_bytes=56 * 1024 * 1024
        ),
        cost_estimate=pl.CostEstimate(
            flops=flops,
            bytes_accessed=4 * shard * (proj + hid),
            transcendentals=2 * count * proj,
        ),
    )(acts_fwd, acts_bwd, cotangent, lens_fwd, lens_bwd, w_proj, w_out[0].T)
    next_acts, prev_grads, grad_proj, grad_out = pl.pallas_call(
        finish,
        out_shape=results,
        in_specs=[hbm] * 4,
        out_specs=(hbm,) * 4,
        scratch_shapes=[dma((4,))],
    )(*outs)
    return next_acts, prev_grads, grad_proj, grad_out.T[None]


def solution(mesh):
    return jax.shard_map(
        per_device,
        mesh=mesh,
        in_specs=(
            P("pipe", "dp", None),
            P("pipe", "dp", None),
            P("pipe", "dp", None),
            P("pipe", "dp", None),
            P("pipe", "dp", None),
            P("pipe", "dp", None),
            P("pipe", None, "dp"),
        ),
        out_specs=(
            P("pipe", "dp", None),
            P("pipe", "dp", None),
            P("pipe", "dp", None),
            P("pipe", None, "dp"),
        ),
        check_vma=False,
    )
```

```python
import functools
import math

import jax
import jax.numpy as jnp
from jax import lax
from jax.experimental import pallas as pl
from jax.experimental.pallas import tpu as pltpu
from jax.sharding import PartitionSpec as P

HEADS = 4
HEAD_DIM = 128
LMAX = 64
EPS = 1e-05
CORES = 2
PARTS = 5
MESH = pl.DeviceIdType.MESH
BF = jnp.bfloat16
F32 = jnp.float32

NN = (((1,), (0,)), ((), ()))
NT = (((1,), (1,)), ((), ()))
TN = (((0,), (0,)), ((), ()))


def dot(a, b, dims=NN):
    return lax.dot_general(a, b, dims, preferred_element_type=F32)


def sigmoid(v):
    return 0.5 + 0.5 * jnp.tanh(0.5 * v)


def layer_norm(values):
    center = values - jnp.mean(values, axis=-1, keepdims=True)
    inverse = lax.rsqrt(jnp.mean(center * center, axis=-1, keepdims=True) + EPS)
    return center * inverse, inverse


def norm_back(grad, normed, inverse):
    return inverse * (
        grad
        - jnp.mean(grad, axis=-1, keepdims=True)
        - normed * jnp.mean(grad * normed, axis=-1, keepdims=True)
    )


def jagged_mask(lens_ref, count):
    rows = lax.broadcasted_iota(jnp.int32, (count, count), 0)
    cols = lax.broadcasted_iota(jnp.int32, (count, count), 1)
    row_seg = jnp.zeros((count, count), jnp.int32)
    col_seg = jnp.zeros((count, count), jnp.int32)
    end = jnp.int32(0)
    for user in range(lens_ref.shape[2]):
        end = end + lens_ref[0, 0, user]
        row_seg += jnp.where(rows >= end, 1, 0)
        col_seg += jnp.where(cols >= end, 1, 0)
    keep = (row_seg == col_seg) & (cols <= rows)
    return jnp.where(keep, 1.0 / LMAX, 0.0)


def kernel(
    chips,
    phases,
    xf_ref,
    xb_ref,
    g_ref,
    lf_ref,
    lb_ref,
    wp_ref,
    wo_ref,
    next_ref,
    prev_ref,
    gp_ref,
    go_ref,
    wall,
    xnf,
    xnb,
    normed_ref,
    norm_t,
    g_t,
    hidden,
    slope,
    gpre,
    gated_b,
    gnorm,
    fwd_out,
    bwd_out,
    own,
    psend,
    precv,
    lrecv,
    rrecv,
    stage,
    ag_right,
    ag_left,
    ag_part,
    ag_chain,
    ag_precv,
    rs_send,
    rs_part,
    rs_precv,
    rs_lrecv,
    rs_rrecv,
    pipe_sems,
):
    val, que, key, gat, out = range(PARTS)
    shard, hid = wo_ref.shape
    count, model = xf_ref.shape[1:]
    scale = HEAD_DIM ** (-0.5)
    loss_scale = 1.0 / math.sqrt(chips * CORES * count)
    me = lax.axis_index("dp")
    phase = lax.axis_index("pipe")
    z, c = lax.div(me, CORES), lax.rem(me, CORES)
    has_left, has_right = z > 0, z < chips - 1
    middle = has_left & has_right
    end = jnp.logical_not(middle)
    left, right, partner = {"dp": me - CORES}, {"dp": me + CORES}, {"dp": z * CORES + 1 - c}
    ahead = {"pipe": lax.rem(phase + 1, phases)}
    behind = {"pipe": lax.rem(phase + phases - 1, phases)}

    barrier = pltpu.get_barrier_semaphore()

    def greet(target):
        pl.semaphore_signal(barrier, inc=1, device_id=target, device_id_type=MESH)

    @pl.when(has_left)
    def _():
        greet(left)

    @pl.when(has_right)
    def _():
        greet(right)

    greet(partner)
    greet(ahead)
    greet(behind)

    def rows(chip, core):
        return pl.ds(pl.multiple_of((chip * CORES + core) * shard, shard), shard)

    def home(i):
        start = (i + 1) % (PARTS - 1) * hid
        return slice(start, start + hid)

    for i in (val, que, key, gat):
        wall[i, rows(z, c), :] = wp_ref[0, :, home(i)].astype(BF)
    wall[out, rows(z, c), :] = wo_ref[...].astype(BF)

    neighbours = 3 + jnp.where(has_left, 1, 0) + jnp.where(has_right, 1, 0)
    pl.semaphore_wait(barrier, neighbours)

    def remote(src, dst, send_sem, recv_sem, target):
        return pltpu.make_async_remote_copy(
            src_ref=src,
            dst_ref=dst,
            send_sem=send_sem,
            recv_sem=recv_sem,
            device_id=target,
            device_id_type=MESH,
        )

    def gather(i, chip, core, send_sem, recv_sem, target):
        block = wall.at[i, rows(chip, core), :]
        return remote(block, block, send_sem.at[i, chip], recv_sem.at[i, chip], target)

    def to_right(i, chip):
        return gather(i, chip, c, ag_right, ag_chain, right)

    def to_left(i, chip):
        return gather(i, chip, c, ag_left, ag_chain, left)

    def to_partner(i, chip):
        return gather(i, chip, c, ag_part, ag_precv, partner)

    def from_partner(i, chip):
        return gather(i, chip, 1 - c, ag_part, ag_precv, partner)

    def start_own(i):
        @pl.when(has_right)
        def _():
            to_right(i, z).start()

        @pl.when(has_left)
        def _():
            to_left(i, z).start()

        to_partner(i, z).start()

    def loop(lower, upper, body):
        def step(i, carry):
            body(i)
            return carry

        lax.fori_loop(lower, upper, step, 0)

    ahead_parts = 2
    loop(0, ahead_parts, start_own)

    @pl.when(end)
    def _():
        loop(ahead_parts, PARTS, start_own)

    normed_b, inverse_b = layer_norm(xb_ref[0].astype(F32))
    normed_ref[...] = normed_b
    xnb[...] = normed_b.astype(BF)
    normed_f, _ = layer_norm(xf_ref[0].astype(F32))
    xnf[...] = normed_f.astype(BF)
    norm_t[...] = normed_b.T.astype(BF)
    g_t[...] = g_ref[0].astype(F32).T.astype(BF)
    keep_b = jagged_mask(lb_ref, count)

    def relay(i):
        def tick(t):
            from_left, from_right = z - t, z + t

            @pl.when(from_left >= 0)
            def _():
                to_right(i, from_left).wait_recv()

                @pl.when(has_right)
                def _():
                    to_right(i, from_left).start()

                to_partner(i, from_left).start()

            @pl.when(from_right < chips)
            def _():
                to_left(i, from_right).wait_recv()

                @pl.when(has_left)
                def _():
                    to_left(i, from_right).start()

                to_partner(i, from_right).start()

        loop(1, chips, tick)

    def arrivals(i):
        loop(0, chips, lambda j: from_partner(i, j).wait_recv())

    def project(x_ref, i, with_slope):
        value = dot(x_ref[...], wall[i])
        sigma = sigmoid(value)
        silu = value * sigma
        hidden[i] = silu.astype(BF)
        if with_slope:
            slope[i] = sigma + silu * (1.0 - sigma)

    def part(i, head):
        return hidden[i, :, head * HEAD_DIM : (head + 1) * HEAD_DIM]

    def attend(keep):
        sigmas, scores, attns, mixed = [], [], [], []
        for head in range(HEADS):
            score = dot(part(que, head), part(key, head), NT) * scale
            sigma = sigmoid(score)
            attn = (score * sigma * keep).astype(BF)
            mixed.append(dot(attn, part(val, head)))
            scores.append(score)
            sigmas.append(sigma)
            attns.append(attn)
        return sigmas, scores, attns, jnp.concatenate(mixed, axis=1)

    def send_forward():
        return remote(fwd_out, next_ref.at[0], pipe_sems.at[2], pipe_sems.at[3], ahead)

    def send_backward():
        return remote(bwd_out, prev_ref.at[0], pipe_sems.at[0], pipe_sems.at[1], behind)

    def forward_block():
        loop(0, PARTS - 1, lambda i: project(xnf, i, False))
        _, _, _, mixed_f = attend(jagged_mask(lf_ref, count))
        gated_f = (layer_norm(mixed_f)[0] * hidden[gat].astype(F32)).astype(BF)
        result = xf_ref[0].astype(F32) + dot(gated_f, wall[out], NT)
        fwd_out[...] = result.astype(BF)
        send_forward().start()

    def part_copy(i, d):
        return remote(psend.at[i, d], precv.at[i, d], rs_part.at[i, d], rs_precv.at[i, d], partner)

    def right_copy(i, d):
        return remote(stage.at[i, d], lrecv.at[i, d], rs_send.at[i, d], rs_lrecv.at[i, d], right)

    def left_copy(i, d):
        return remote(stage.at[i, d], rrecv.at[i, d], rs_send.at[i, d], rs_rrecv.at[i, d], left)

    def terms(i):
        sides, factor = (g_t, gated_b[...]) if i == out else (norm_t, gpre[i])

        def term(k):
            d = jnp.where(z < chips // 2, chips - 1 - k, k)
            psend[i, d] = (dot(sides[rows(d, 1 - c), :], factor) * loss_scale).astype(BF)
            part_copy(i, d).start()
            own[i, d] = dot(sides[rows(d, c), :], factor) * loss_scale

        loop(0, chips, term)

    def chip_sum(i, d):
        part_copy(i, d).wait_recv()
        return own[i, d] + precv[i, d].astype(F32)

    def reduce(i):
        def tick(tau):
            @pl.when(has_right & (tau >= z))
            def _():
                d = chips - 1 - tau + z
                own[i, d] = chip_sum(i, d)

                @pl.when(has_left)
                def _():
                    right_copy(i, d).wait_recv()
                    own[i, d] = own[i, d] + lrecv[i, d].astype(F32)

                stage[i, d] = own[i, d].astype(BF)
                right_copy(i, d).start()

            @pl.when(has_left & (tau >= chips - 1 - z))
            def _():
                d = tau - (chips - 1 - z)
                own[i, d] = chip_sum(i, d)

                @pl.when(has_right)
                def _():
                    left_copy(i, d).wait_recv()
                    own[i, d] = own[i, d] + rrecv[i, d].astype(F32)

                stage[i, d] = own[i, d].astype(BF)
                left_copy(i, d).start()

        loop(0, chips - 1, tick)

    @pl.when(middle)
    def _():
        def pass_on(i):
            relay(i)

            @pl.when(i + ahead_parts < PARTS)
            def _():
                start_own(i + ahead_parts)

        loop(0, PARTS, pass_on)
        loop(0, PARTS, arrivals)
        forward_block()

    @pl.when(end)
    def _():
        loop(0, gat, relay)
        loop(0, gat, arrivals)

    loop(0, gat, lambda i: project(xnb, i, True))
    sigmas, scores, attns, mixed = attend(keep_b)
    mixed_n, inverse_o = layer_norm(mixed)

    @pl.when(end)
    def _():
        relay(gat)
        arrivals(gat)

    project(xnb, gat, True)
    gate = hidden[gat].astype(F32)
    gated_b[...] = (mixed_n * gate).astype(BF)
    terms(out)

    @pl.when(end)
    def _():
        reduce(out)
        relay(out)
        arrivals(out)

    grad_y = dot(g_ref[0], wall[out])
    gpre[gat] = (grad_y * mixed_n * slope[gat]).astype(BF)
    terms(gat)
    grad_mixed = norm_back(grad_y * gate, mixed_n, inverse_o).astype(BF)
    heads = [slice(head * HEAD_DIM, (head + 1) * HEAD_DIM) for head in range(HEADS)]
    for head, cols in enumerate(heads):
        grad_vals = dot(attns[head], grad_mixed[:, cols], TN)
        gpre[val, :, cols] = (grad_vals * slope[val, :, cols]).astype(BF)
    terms(val)

    @pl.when(end)
    def _():
        reduce(gat)

    for head, cols in enumerate(heads):
        score, sigma = scores[head], sigmas[head]
        grad_attn = dot(grad_mixed[:, cols], part(val, head), NT)
        grad_s = (
            grad_attn * keep_b * (sigma * (1.0 + score * (1.0 - sigma))) * scale
        ).astype(BF)
        grad_q = dot(grad_s, part(key, head))
        grad_k = dot(grad_s, part(que, head), TN)
        gpre[que, :, cols] = (grad_q * slope[que, :, cols]).astype(BF)
        gpre[key, :, cols] = (grad_k * slope[key, :, cols]).astype(BF)
    terms(que)

    @pl.when(end)
    def _():
        reduce(val)

    terms(key)

    @pl.when(end)
    def _():
        reduce(que)
        reduce(key)

    @pl.when(middle)
    def _():
        reduce(out)
        reduce(gat)

    row_tile = 256

    def norm_grad(n):
        at = pl.ds(pl.multiple_of(n * row_tile, row_tile), row_tile)
        total = dot(gpre[val], wall[val, at, :], NT)
        for i in (que, key, gat):
            total += dot(gpre[i], wall[i, at, :], NT)
        gnorm[:, at] = total

    loop(0, model // row_tile, norm_grad)
    grad_in = g_ref[0].astype(F32) + norm_back(gnorm[...], normed_ref[...], inverse_b)
    bwd_out[...] = grad_in.astype(BF)
    send_backward().start()

    @pl.when(middle)
    def _():
        reduce(val)
        reduce(que)
        reduce(key)

    @pl.when(end)
    def _():
        forward_block()

    for i in (out, gat, val, que, key):
        own[i, z] = chip_sum(i, z)

        @pl.when(has_left)
        def _():
            right_copy(i, z).wait_recv()
            own[i, z] = own[i, z] + lrecv[i, z].astype(F32)

        @pl.when(has_right)
        def _():
            left_copy(i, z).wait_recv()
            own[i, z] = own[i, z] + rrecv[i, z].astype(F32)

        if i == out:
            go_ref[...] = own[i, z]
        else:
            gp_ref[0, :, home(i)] = own[i, z]

    send_backward().wait()
    send_forward().wait()

    def drain(j):
        def each(i):
            to_partner(i, j).wait_send()
            part_copy(i, j).wait_send()

            @pl.when(has_right & (j <= z))
            def _():
                to_right(i, j).wait_send()

            @pl.when(has_left & (j >= z))
            def _():
                to_left(i, j).wait_send()

            @pl.when(j != z)
            def _():
                right_copy(i, j).wait_send()

        loop(0, PARTS, each)

    loop(0, chips, drain)


def finish(*refs):
    half = len(refs) // 2
    for src, dst in zip(refs[:half], refs[half:]):
        dst[...] = src[...]


def per_device(acts_fwd, acts_bwd, cotangent, lens_fwd, lens_bwd, w_proj, w_out):
    chips = lax.axis_size("dp") // CORES
    phases = lax.axis_size("pipe")
    _, count, model = acts_fwd.shape
    _, shard, proj = w_proj.shape
    hid = w_out.shape[1]
    vmem = pl.BlockSpec(memory_space=pltpu.VMEM)
    smem = pl.BlockSpec(memory_space=pltpu.SMEM)
    dma = pltpu.SemaphoreType.DMA
    slots = pltpu.VMEM((PARTS, chips, shard, hid), BF)
    flops = 2 * count * model * (2 * proj + 2 * proj + 4 * hid)
    results = (
        jax.ShapeDtypeStruct((1, count, model), BF),
        jax.ShapeDtypeStruct((1, count, model), BF),
        jax.ShapeDtypeStruct((1, shard, proj), F32),
        jax.ShapeDtypeStruct((shard, hid), F32),
    )
    outs = pl.pallas_call(
        functools.partial(kernel, chips, phases),
        out_shape=results,
        in_specs=[vmem, vmem, vmem, smem, smem, vmem, vmem],
        out_specs=(vmem, vmem, vmem, vmem),
        scratch_shapes=[
            pltpu.VMEM((PARTS, model, hid), BF),
            pltpu.VMEM((count, model), BF),
            pltpu.VMEM((count, model), BF),
            pltpu.VMEM((count, model), F32),
            pltpu.VMEM((model, count), BF),
            pltpu.VMEM((model, count), BF),
            pltpu.VMEM((PARTS - 1, count, hid), BF),
            pltpu.VMEM((PARTS - 1, count, hid), F32),
            pltpu.VMEM((PARTS - 1, count, hid), BF),
            pltpu.VMEM((count, hid), BF),
            pltpu.VMEM((count, model), F32),
            pltpu.VMEM((count, model), BF),
            pltpu.VMEM((count, model), BF),
            pltpu.VMEM((PARTS, chips, shard, hid), F32),
            slots,
            slots,
            slots,
            slots,
            slots,
        ]
        + [dma((PARTS, chips))] * 10
        + [dma((4,))],
        compiler_params=pltpu.CompilerParams(
            collective_id=0, has_side_effects=True, vmem_limit_bytes=56 * 1024 * 1024
        ),
        cost_estimate=pl.CostEstimate(
            flops=flops,
            bytes_accessed=4 * shard * (proj + hid),
            transcendentals=2 * count * proj,
        ),
    )(acts_fwd, acts_bwd, cotangent, lens_fwd, lens_bwd, w_proj, w_out[0].T)
    next_acts, prev_grads, grad_proj, grad_out = pl.pallas_call(
        finish,
        out_shape=results,
        in_specs=[vmem] * 4,
        out_specs=(vmem,) * 4,
    )(*outs)
    return next_acts, prev_grads, grad_proj, grad_out.T[None]


def solution(mesh):
    return jax.shard_map(
        per_device,
        mesh=mesh,
        in_specs=(
            P("pipe", "dp", None),
            P("pipe", "dp", None),
            P("pipe", "dp", None),
            P("pipe", "dp", None),
            P("pipe", "dp", None),
            P("pipe", "dp", None),
            P("pipe", None, "dp"),
        ),
        out_specs=(
            P("pipe", "dp", None),
            P("pipe", "dp", None),
            P("pipe", "dp", None),
            P("pipe", None, "dp"),
        ),
        check_vma=False,
    )
```

```python
import functools
import math

import jax
import jax.numpy as jnp
from jax import lax
from jax.experimental import pallas as pl
from jax.experimental.pallas import tpu as pltpu
from jax.sharding import PartitionSpec as P

HEADS = 4
HEAD_DIM = 128
LMAX = 64
EPS = 1e-05
CORES = 2
PARTS = 5
MESH = pl.DeviceIdType.MESH
BF = jnp.bfloat16
F32 = jnp.float32

NN = (((1,), (0,)), ((), ()))
NT = (((1,), (1,)), ((), ()))
TN = (((0,), (0,)), ((), ()))


def dot(a, b, dims=NN):
    return lax.dot_general(a, b, dims, preferred_element_type=F32)


def sigmoid(v):
    return 0.5 + 0.5 * jnp.tanh(0.5 * v)


def layer_norm(values):
    center = values - jnp.mean(values, axis=-1, keepdims=True)
    inverse = lax.rsqrt(jnp.mean(center * center, axis=-1, keepdims=True) + EPS)
    return center * inverse, inverse


def norm_back(grad, normed, inverse):
    return inverse * (
        grad
        - jnp.mean(grad, axis=-1, keepdims=True)
        - normed * jnp.mean(grad * normed, axis=-1, keepdims=True)
    )


def jagged_mask(lens_ref, count):
    rows = lax.broadcasted_iota(jnp.int32, (count, count), 0)
    cols = lax.broadcasted_iota(jnp.int32, (count, count), 1)
    row_seg = jnp.zeros((count, count), jnp.int32)
    col_seg = jnp.zeros((count, count), jnp.int32)
    end = jnp.int32(0)
    for user in range(lens_ref.shape[2]):
        end = end + lens_ref[0, 0, user]
        row_seg += jnp.where(rows >= end, 1, 0)
        col_seg += jnp.where(cols >= end, 1, 0)
    keep = (row_seg == col_seg) & (cols <= rows)
    return jnp.where(keep, 1.0 / LMAX, 0.0)


def kernel(
    chips,
    phases,
    xf_ref,
    xb_ref,
    g_ref,
    lf_ref,
    lb_ref,
    wp_ref,
    wo_ref,
    next_ref,
    prev_ref,
    gp_ref,
    go_ref,
    wall,
    xnf,
    xnb,
    normed_ref,
    norm_t,
    g_both,
    g_t,
    hidden,
    slope,
    gpre,
    gated_b,
    gnorm,
    fwd_out,
    bwd_out,
    own,
    psend,
    precv,
    lrecv,
    rrecv,
    stage,
    final,
    masks,
    mate_acts,
    mate_masks,
    ag_right,
    ag_left,
    ag_part,
    ag_chain,
    ag_precv,
    rs_send,
    rs_part,
    rs_precv,
    rs_lrecv,
    rs_rrecv,
    fin_send,
    fin_recv,
    act_send,
    act_recv,
    pipe_send,
    pipe_recv,
):
    val, que, key, gat, out = range(PARTS)
    shard, hid = wo_ref.shape
    count, model = xf_ref.shape[1:]
    scale = HEAD_DIM ** (-0.5)
    loss_scale = 1.0 / math.sqrt(chips * CORES * count)
    me = lax.axis_index("dp")
    phase = lax.axis_index("pipe")
    z, c = lax.div(me, CORES), lax.rem(me, CORES)

    pairs = chips // 2
    m = lax.div(z, 2)

    def inner(pair):
        return 2 * pair + jnp.where(2 * pair < pairs, 1, 0)

    worker = z == inner(m)
    helper = jnp.logical_not(worker)
    other = 4 * m + 1 - z
    has_left, has_right = m > 0, m < pairs - 1
    mate_dp = other * CORES + c
    mate, partner = {"dp": mate_dp}, {"dp": z * CORES + 1 - c}
    left, right = {"dp": inner(m - 1) * CORES + c}, {"dp": inner(m + 1) * CORES + c}
    ahead = lax.rem(phase + 1, phases)
    behind = lax.rem(phase + phases - 1, phases)

    barrier = pltpu.get_barrier_semaphore()

    def greet(target):
        pl.semaphore_signal(barrier, inc=1, device_id=target, device_id_type=MESH)

    greet(mate)

    @pl.when(helper)
    def _():
        greet({"dp": mate_dp, "pipe": ahead})
        greet({"dp": mate_dp, "pipe": behind})

    @pl.when(worker)
    def _():
        greet(partner)
        greet({"pipe": ahead})
        greet({"pipe": behind})

        @pl.when(has_left)
        def _():
            greet(left)

        @pl.when(has_right)
        def _():
            greet(right)

    def rows(chip, core):
        return pl.ds(pl.multiple_of((chip * CORES + core) * shard, shard), shard)

    def home(i):
        start = (i + 1) % (PARTS - 1) * hid
        return slice(start, start + hid)

    for i in (val, que, key, gat):
        wall[i, rows(z, c), :] = wp_ref[0, :, home(i)].astype(BF)
    wall[out, rows(z, c), :] = wo_ref[...].astype(BF)

    peers = jnp.where(worker, 6 + jnp.where(has_left, 1, 0) + jnp.where(has_right, 1, 0), 1)
    pl.semaphore_wait(barrier, peers)

    def remote(src, dst, send_sem, recv_sem, target):
        return pltpu.make_async_remote_copy(
            src_ref=src,
            dst_ref=dst,
            send_sem=send_sem,
            recv_sem=recv_sem,
            device_id=target,
            device_id_type=MESH,
        )

    def gather(i, chip, core, send_sem, recv_sem, target):
        block = wall.at[i, rows(chip, core), :]
        return remote(block, block, send_sem.at[i, chip], recv_sem.at[i, chip], target)

    def to_right(i, chip):
        return gather(i, chip, c, ag_right, ag_chain, right)

    def to_left(i, chip):
        return gather(i, chip, c, ag_left, ag_chain, left)

    def to_mate(i):
        return gather(i, z, c, ag_right, ag_chain, mate)

    def to_partner(i, chip):
        return gather(i, chip, c, ag_part, ag_precv, partner)

    def from_partner(i, chip):
        return gather(i, chip, 1 - c, ag_part, ag_precv, partner)

    def act_copy(n):
        src, dst = (
            (xb_ref.at[0], mate_acts.at[0]),
            (masks, mate_masks),
            (g_ref.at[0], mate_acts.at[1]),
            (xf_ref.at[0], mate_acts.at[2]),
        )[n]
        return remote(src, dst, act_send.at[n], act_recv.at[n], mate)

    def final_copy(i):
        return remote(stage.at[i, other], final.at[i], fin_send.at[i], fin_recv.at[i], mate)

    def out_copy(n, to_mate_block):
        source, target_ref, to = ((fwd_out, next_ref, ahead), (bwd_out, prev_ref, behind))[n]
        src = source.at[pl.ds(count, count) if to_mate_block else pl.ds(0, count)]
        send = pipe_send.at[2 * n + (1 if to_mate_block else 0)]
        target = {"dp": mate_dp, "pipe": to} if to_mate_block else {"pipe": to}
        return remote(src, target_ref.at[0], send, pipe_recv.at[n], target)

    def loop(lower, upper, body):
        def step(i, carry):
            body(i)
            return carry

        lax.fori_loop(lower, upper, step, 0)

    @pl.when(helper)
    def _():
        to_mate(0).start()
        to_mate(1).start()
        act_copy(0).start()
        masks[0] = jagged_mask(lb_ref, count).astype(BF)
        masks[1] = jagged_mask(lf_ref, count).astype(BF)
        act_copy(1).start()
        for i in range(2, PARTS):
            to_mate(i).start()
        act_copy(2).start()
        act_copy(3).start()

        for i in (out, gat, val, que, key):
            final_copy(i).wait_recv()
            if i == out:
                go_ref[...] = final[i].astype(F32)
            else:
                gp_ref[0, :, home(i)] = final[i].astype(F32)
        for n in range(4):
            act_copy(n).wait_send()
        for i in range(PARTS):
            to_mate(i).wait_send()

    @pl.when(worker)
    def _():
        def send_on(i, chip):
            @pl.when(has_right)
            def _():
                to_right(i, chip).start()

            @pl.when(has_left)
            def _():
                to_left(i, chip).start()

            to_partner(i, chip).start()

        early = 2
        loop(0, early, lambda i: send_on(i, z))

        first, second = slice(0, count), slice(count, 2 * count)

        def prepare(at, tokens):
            normed, inverse = layer_norm(tokens.astype(F32))
            normed_ref[at, :] = normed
            xnb[at, :] = normed.astype(BF)
            norm_t[:, at] = normed.T.astype(BF)
            return inverse

        inverse_own = prepare(first, xb_ref[0])

        def mate_part(i):
            to_left(i, other).wait_recv()
            send_on(i, other)

            @pl.when(i + early < PARTS)
            def _():
                send_on(i + early, z)

        def line(i):
            def tick(t):
                lower, upper = m - t, m + t

                @pl.when(lower >= 0)
                def _():
                    for chip in (2 * lower, 2 * lower + 1):
                        to_right(i, chip).wait_recv()

                        @pl.when(has_right)
                        def _():
                            to_right(i, chip).start()

                        to_partner(i, chip).start()

                @pl.when(upper < pairs)
                def _():
                    for chip in (2 * upper, 2 * upper + 1):
                        to_left(i, chip).wait_recv()

                        @pl.when(has_left)
                        def _():
                            to_left(i, chip).start()

                        to_partner(i, chip).start()

            loop(1, pairs, tick)

        def arrivals(i):
            loop(0, chips, lambda j: from_partner(i, j).wait_recv())

        loop(0, PARTS, mate_part)

        act_copy(0).wait_recv()
        inverse_mate = prepare(second, mate_acts[0])
        inverse_b = jnp.concatenate([inverse_own, inverse_mate], axis=0)
        g_both[first, :] = g_ref[0]
        g_t[:, first] = g_ref[0].astype(F32).T.astype(BF)
        xnf[first, :] = layer_norm(xf_ref[0].astype(F32))[0].astype(BF)
        act_copy(1).wait_recv()
        keeps_b = [jagged_mask(lb_ref, count), mate_masks[0].astype(F32)]

        def project(x_ref, i, with_slope):
            value = dot(x_ref[...], wall[i])
            sigma = sigmoid(value)
            silu = value * sigma
            hidden[i] = silu.astype(BF)
            if with_slope:
                slope[i] = sigma + silu * (1.0 - sigma)

        heads = [slice(head * HEAD_DIM, (head + 1) * HEAD_DIM) for head in range(HEADS)]

        def attend(keeps):
            sigmas, scores, attns, blocks = [], [], [], []
            for at, keep in zip((first, second), keeps):
                mixed = []
                for cols in heads:
                    score = dot(hidden[que, at, cols], hidden[key, at, cols], NT) * scale
                    sigma = sigmoid(score)
                    attn = (score * sigma * keep).astype(BF)
                    mixed.append(dot(attn, hidden[val, at, cols]))
                    scores.append(score)
                    sigmas.append(sigma)
                    attns.append(attn)
                blocks.append(jnp.concatenate(mixed, axis=1))
            return sigmas, scores, attns, jnp.concatenate(blocks, axis=0)

        def both(pair):
            return pl.ds(2 * pair, 2)

        def part_copy(i, j):
            return remote(
                psend.at[i, both(j)], precv.at[i, both(j)], rs_part.at[i, j], rs_precv.at[i, j], partner
            )

        def right_copy(i, j):
            return remote(
                stage.at[i, both(j)], lrecv.at[i, both(j)], rs_send.at[i, j], rs_lrecv.at[i, j], right
            )

        def left_copy(i, j):
            return remote(
                stage.at[i, both(j)], rrecv.at[i, both(j)], rs_send.at[i, j], rs_rrecv.at[i, j], left
            )

        def terms(i):
            sides, factor = (g_t, gated_b[...]) if i == out else (norm_t, gpre[i])

            def term(k):
                j = jnp.where(2 * m < pairs, pairs - 1 - k, k)
                for d in (2 * j, 2 * j + 1):
                    theirs = dot(sides[rows(d, 1 - c), :], factor) * loss_scale
                    psend[i, d] = theirs.astype(BF)
                part_copy(i, j).start()
                for d in (2 * j, 2 * j + 1):
                    own[i, d] = dot(sides[rows(d, c), :], factor) * loss_scale

            loop(0, pairs, term)

        def chip_sum(i, j):
            part_copy(i, j).wait_recv()
            at = both(j)
            own[i, at] = own[i, at] + precv[i, at].astype(F32)

        def add_left(i, j):
            right_copy(i, j).wait_recv()
            own[i, both(j)] = own[i, both(j)] + lrecv[i, both(j)].astype(F32)

        def add_right(i, j):
            left_copy(i, j).wait_recv()
            own[i, both(j)] = own[i, both(j)] + rrecv[i, both(j)].astype(F32)

        def reduce(i):
            def tick(tau):
                @pl.when(has_right & (tau >= m))
                def _():
                    j = pairs - 1 - tau + m
                    chip_sum(i, j)

                    @pl.when(has_left)
                    def _():
                        add_left(i, j)

                    stage[i, both(j)] = own[i, both(j)].astype(BF)
                    right_copy(i, j).start()

                @pl.when(has_left & (tau >= pairs - 1 - m))
                def _():
                    j = tau - (pairs - 1 - m)
                    chip_sum(i, j)

                    @pl.when(has_right)
                    def _():
                        add_right(i, j)

                    stage[i, both(j)] = own[i, both(j)].astype(BF)
                    left_copy(i, j).start()

            loop(0, pairs - 1, tick)

        def conclude(i):
            chip_sum(i, m)

            @pl.when(has_left)
            def _():
                add_left(i, m)

            @pl.when(has_right)
            def _():
                add_right(i, m)

            stage[i, other] = own[i, other].astype(BF)
            final_copy(i).start()
            if i == out:
                go_ref[...] = own[i, z]
            else:
                gp_ref[0, :, home(i)] = own[i, z]

        loop(0, gat, line)
        loop(0, gat, arrivals)
        loop(0, gat, lambda i: project(xnb, i, True))
        line(gat)
        sigmas, scores, attns, mixed = attend(keeps_b)
        mixed_n, inverse_o = layer_norm(mixed)
        arrivals(gat)
        project(xnb, gat, True)
        gate = hidden[gat].astype(F32)
        gated_b[...] = (mixed_n * gate).astype(BF)
        act_copy(2).wait_recv()
        g_both[second, :] = mate_acts[1]
        g_t[:, second] = mate_acts[1].astype(F32).T.astype(BF)
        terms(out)
        line(out)
        reduce(out)
        arrivals(out)

        grad_y = dot(g_both[...], wall[out])
        gpre[gat] = (grad_y * mixed_n * slope[gat]).astype(BF)
        terms(gat)
        grad_mixed = norm_back(grad_y * gate, mixed_n, inverse_o).astype(BF)
        reduce(gat)
        blocks = [(b, at, n, cols) for b, at in enumerate((first, second)) for n, cols in enumerate(heads)]
        for b, at, n, cols in blocks:
            grad_vals = dot(attns[b * HEADS + n], grad_mixed[at, cols], TN)
            gpre[val, at, cols] = (grad_vals * slope[val, at, cols]).astype(BF)
        terms(val)
        for b, at, n, cols in blocks:
            score, sigma = scores[b * HEADS + n], sigmas[b * HEADS + n]
            grad_attn = dot(grad_mixed[at, cols], hidden[val, at, cols], NT)
            grad_s = (
                grad_attn * keeps_b[b] * (sigma * (1.0 + score * (1.0 - sigma))) * scale
            ).astype(BF)
            grad_q = dot(grad_s, hidden[key, at, cols])
            grad_k = dot(grad_s, hidden[que, at, cols], TN)
            gpre[que, at, cols] = (grad_q * slope[que, at, cols]).astype(BF)
            gpre[key, at, cols] = (grad_k * slope[key, at, cols]).astype(BF)
        reduce(val)
        terms(que)
        terms(key)
        reduce(que)
        reduce(key)

        row_tile = 256

        def norm_grad(n):
            at = pl.ds(pl.multiple_of(n * row_tile, row_tile), row_tile)
            total = dot(gpre[val], wall[val, at, :], NT)
            for i in (que, key, gat):
                total += dot(gpre[i], wall[i, at, :], NT)
            gnorm[:, at] = total

        loop(0, model // row_tile, norm_grad)
        grad_in = g_both[...].astype(F32) + norm_back(gnorm[...], normed_ref[...], inverse_b)
        bwd_out[...] = grad_in.astype(BF)
        out_copy(1, True).start()
        out_copy(1, False).start()
        conclude(out)

        act_copy(3).wait_recv()
        xnf[second, :] = layer_norm(mate_acts[2].astype(F32))[0].astype(BF)
        loop(0, PARTS - 1, lambda i: project(xnf, i, False))
        conclude(gat)
        keeps_f = [jagged_mask(lf_ref, count), mate_masks[1].astype(F32)]
        mixed_f = attend(keeps_f)[3]
        gated_f = (layer_norm(mixed_f)[0] * hidden[gat].astype(F32)).astype(BF)
        conclude(val)
        change = dot(gated_f, wall[out], NT)
        fwd_out[second, :] = (mate_acts[2].astype(F32) + change[second]).astype(BF)
        out_copy(0, True).start()
        fwd_out[first, :] = (xf_ref[0].astype(F32) + change[first]).astype(BF)
        out_copy(0, False).start()
        conclude(que)
        conclude(key)

        for n in range(2):
            out_copy(n, True).wait_send()
            out_copy(n, False).wait_send()

        def drain(i):
            final_copy(i).wait_send()

            def each(j):
                to_partner(i, j).wait_send()

                @pl.when(has_right & (lax.div(j, 2) <= m))
                def _():
                    to_right(i, j).wait_send()

                @pl.when(has_left & (lax.div(j, 2) >= m))
                def _():
                    to_left(i, j).wait_send()

            loop(0, chips, each)

            def pair_sends(j):
                part_copy(i, j).wait_send()

                @pl.when(j != m)
                def _():
                    right_copy(i, j).wait_send()

            loop(0, pairs, pair_sends)

        loop(0, PARTS, drain)

    for n in range(2):
        out_copy(n, False).wait_recv()


def finish(*refs):
    half = len(refs) // 2
    for src, dst in zip(refs[:half], refs[half:]):
        dst[...] = src[...]


def per_device(acts_fwd, acts_bwd, cotangent, lens_fwd, lens_bwd, w_proj, w_out):
    chips = lax.axis_size("dp") // CORES
    phases = lax.axis_size("pipe")
    _, count, model = acts_fwd.shape
    _, shard, proj = w_proj.shape
    hid = w_out.shape[1]
    vmem = pl.BlockSpec(memory_space=pltpu.VMEM)
    smem = pl.BlockSpec(memory_space=pltpu.SMEM)
    dma = pltpu.SemaphoreType.DMA
    slots = pltpu.VMEM((PARTS, chips, shard, hid), BF)
    flops = 2 * count * model * (2 * proj + 2 * proj + 4 * hid)
    results = (
        jax.ShapeDtypeStruct((1, count, model), BF),
        jax.ShapeDtypeStruct((1, count, model), BF),
        jax.ShapeDtypeStruct((1, shard, proj), F32),
        jax.ShapeDtypeStruct((shard, hid), F32),
    )
    outs = pl.pallas_call(
        functools.partial(kernel, chips, phases),
        out_shape=results,
        in_specs=[vmem, vmem, vmem, smem, smem, vmem, vmem],
        out_specs=(vmem, vmem, vmem, vmem),
        scratch_shapes=[
            pltpu.VMEM((PARTS, model, hid), BF),
            pltpu.VMEM((2 * count, model), BF),
            pltpu.VMEM((2 * count, model), BF),
            pltpu.VMEM((2 * count, model), F32),
            pltpu.VMEM((model, 2 * count), BF),
            pltpu.VMEM((2 * count, model), BF),
            pltpu.VMEM((model, 2 * count), BF),
            pltpu.VMEM((PARTS - 1, 2 * count, hid), BF),
            pltpu.VMEM((PARTS - 1, 2 * count, hid), F32),
            pltpu.VMEM((PARTS - 1, 2 * count, hid), BF),
            pltpu.VMEM((2 * count, hid), BF),
            pltpu.VMEM((2 * count, model), F32),
            pltpu.VMEM((2 * count, model), BF),
            pltpu.VMEM((2 * count, model), BF),
            pltpu.VMEM((PARTS, chips, shard, hid), F32),
            slots,
            slots,
            slots,
            slots,
            slots,
            pltpu.VMEM((PARTS, shard, hid), BF),
            pltpu.VMEM((2, count, count), BF),
            pltpu.VMEM((3, count, model), BF),
            pltpu.VMEM((2, count, count), BF),
        ]
        + [dma((PARTS, chips))] * 5
        + [dma((PARTS, chips // 2))] * 5
        + [dma((PARTS,))] * 2
        + [dma((4,))] * 3
        + [dma((2,))],
        compiler_params=pltpu.CompilerParams(
            collective_id=0, has_side_effects=True, vmem_limit_bytes=56 * 1024 * 1024
        ),
        cost_estimate=pl.CostEstimate(
            flops=flops,
            bytes_accessed=4 * shard * (proj + hid),
            transcendentals=2 * count * proj,
        ),
    )(acts_fwd, acts_bwd, cotangent, lens_fwd, lens_bwd, w_proj, w_out[0].T)
    next_acts, prev_grads, grad_proj, grad_out = pl.pallas_call(
        finish,
        out_shape=results,
        in_specs=[vmem] * 4,
        out_specs=(vmem,) * 4,
    )(*outs)
    return next_acts, prev_grads, grad_proj, grad_out.T[None]


def solution(mesh):
    return jax.shard_map(
        per_device,
        mesh=mesh,
        in_specs=(
            P("pipe", "dp", None),
            P("pipe", "dp", None),
            P("pipe", "dp", None),
            P("pipe", "dp", None),
            P("pipe", "dp", None),
            P("pipe", "dp", None),
            P("pipe", None, "dp"),
        ),
        out_specs=(
            P("pipe", "dp", None),
            P("pipe", "dp", None),
            P("pipe", "dp", None),
            P("pipe", None, "dp"),
        ),
        check_vma=False,
    )
```

```python
import functools
import math

import jax
import jax.numpy as jnp
from jax import lax
from jax.experimental import pallas as pl
from jax.experimental.pallas import tpu as pltpu
from jax.sharding import PartitionSpec as P

HEADS = 4
HEAD_DIM = 128
LMAX = 64
EPS = 1e-05
CORES = 2
PARTS = 5
MESH = pl.DeviceIdType.MESH
BF = jnp.bfloat16
F32 = jnp.float32

NN = (((1,), (0,)), ((), ()))
NT = (((1,), (1,)), ((), ()))
TN = (((0,), (0,)), ((), ()))


def dot(a, b, dims=NN):
    return lax.dot_general(a, b, dims, preferred_element_type=F32)


def sigmoid(v):
    return 0.5 + 0.5 * jnp.tanh(0.5 * v)


def layer_norm(values):
    center = values - jnp.mean(values, axis=-1, keepdims=True)
    inverse = lax.rsqrt(jnp.mean(center * center, axis=-1, keepdims=True) + EPS)
    return center * inverse, inverse


def norm_back(grad, normed, inverse):
    return inverse * (
        grad
        - jnp.mean(grad, axis=-1, keepdims=True)
        - normed * jnp.mean(grad * normed, axis=-1, keepdims=True)
    )


def jagged_mask(lens_ref, count):
    rows = lax.broadcasted_iota(jnp.int32, (count, count), 0)
    cols = lax.broadcasted_iota(jnp.int32, (count, count), 1)
    row_seg = jnp.zeros((count, count), jnp.int32)
    col_seg = jnp.zeros((count, count), jnp.int32)
    end = jnp.int32(0)
    for user in range(lens_ref.shape[2]):
        end = end + lens_ref[0, 0, user]
        row_seg += jnp.where(rows >= end, 1, 0)
        col_seg += jnp.where(cols >= end, 1, 0)
    keep = (row_seg == col_seg) & (cols <= rows)
    return jnp.where(keep, 1.0 / LMAX, 0.0)


def kernel(
    chips,
    phases,
    xf_ref,
    xb_ref,
    g_ref,
    lf_ref,
    lb_ref,
    wp_ref,
    wo_ref,
    next_ref,
    prev_ref,
    gp_ref,
    go_ref,
    wall,
    xnf,
    xnb,
    normed_ref,
    norm_t,
    g_both,
    g_t,
    hidden,
    hidden_f,
    slope,
    gpre,
    gated_b,
    gnorm,
    fwd_out,
    bwd_out,
    own,
    psend,
    precv,
    lrecv,
    rrecv,
    stage,
    final,
    masks,
    mate_acts,
    mate_masks,
    ag_right,
    ag_left,
    ag_part,
    ag_chain,
    ag_precv,
    rs_send,
    rs_part,
    rs_precv,
    rs_lrecv,
    rs_rrecv,
    fin_send,
    fin_recv,
    act_send,
    act_recv,
    pipe_send,
    pipe_recv,
):
    val, que, key, gat, out = range(PARTS)
    shard, hid = wo_ref.shape
    count, model = xf_ref.shape[1:]
    scale = HEAD_DIM ** (-0.5)
    loss_scale = 1.0 / math.sqrt(chips * CORES * count)
    me = lax.axis_index("dp")
    phase = lax.axis_index("pipe")
    z, c = lax.div(me, CORES), lax.rem(me, CORES)

    pairs = chips // 2
    m = lax.div(z, 2)

    def inner(pair):
        return 2 * pair + jnp.where(2 * pair < pairs, 1, 0)

    worker = z == inner(m)
    helper = jnp.logical_not(worker)
    other = 4 * m + 1 - z
    has_left, has_right = m > 0, m < pairs - 1
    mate_dp = other * CORES + c
    mate, partner = {"dp": mate_dp}, {"dp": z * CORES + 1 - c}
    left, right = {"dp": inner(m - 1) * CORES + c}, {"dp": inner(m + 1) * CORES + c}
    ahead = lax.rem(phase + 1, phases)
    behind = lax.rem(phase + phases - 1, phases)

    barrier = pltpu.get_barrier_semaphore()

    def greet(target):
        pl.semaphore_signal(barrier, inc=1, device_id=target, device_id_type=MESH)

    greet(mate)

    @pl.when(helper)
    def _():
        greet({"dp": mate_dp, "pipe": ahead})
        greet({"dp": mate_dp, "pipe": behind})

    @pl.when(worker)
    def _():
        greet(partner)
        greet({"pipe": ahead})
        greet({"pipe": behind})

        @pl.when(has_left)
        def _():
            greet(left)

        @pl.when(has_right)
        def _():
            greet(right)

    def rows(chip, core):
        return pl.ds(pl.multiple_of((chip * CORES + core) * shard, shard), shard)

    def home(i):
        start = (i + 1) % (PARTS - 1) * hid
        return slice(start, start + hid)

    for i in (val, que, key, gat):
        wall[i, rows(z, c), :] = wp_ref[0, :, home(i)].astype(BF)
    wall[out, rows(z, c), :] = wo_ref[...].astype(BF)

    peers = jnp.where(worker, 6 + jnp.where(has_left, 1, 0) + jnp.where(has_right, 1, 0), 1)
    pl.semaphore_wait(barrier, peers)

    def remote(src, dst, send_sem, recv_sem, target):
        return pltpu.make_async_remote_copy(
            src_ref=src,
            dst_ref=dst,
            send_sem=send_sem,
            recv_sem=recv_sem,
            device_id=target,
            device_id_type=MESH,
        )

    def gather(i, chip, core, send_sem, recv_sem, target):
        block = wall.at[i, rows(chip, core), :]
        return remote(block, block, send_sem.at[i, chip], recv_sem.at[i, chip], target)

    def to_right(i, chip):
        return gather(i, chip, c, ag_right, ag_chain, right)

    def to_left(i, chip):
        return gather(i, chip, c, ag_left, ag_chain, left)

    def to_mate(i):
        return gather(i, z, c, ag_right, ag_chain, mate)

    def to_partner(i, chip):
        return gather(i, chip, c, ag_part, ag_precv, partner)

    def from_partner(i, chip):
        return gather(i, chip, 1 - c, ag_part, ag_precv, partner)

    def act_copy(n):
        src, dst = (
            (xb_ref.at[0], mate_acts.at[0]),
            (masks, mate_masks),
            (g_ref.at[0], mate_acts.at[1]),
            (xf_ref.at[0], mate_acts.at[2]),
        )[n]
        return remote(src, dst, act_send.at[n], act_recv.at[n], mate)

    def final_copy(i):
        return remote(stage.at[i, other], final.at[i], fin_send.at[i], fin_recv.at[i], mate)

    def out_copy(n, to_mate_block):
        source, target_ref, to = ((fwd_out, next_ref, ahead), (bwd_out, prev_ref, behind))[n]
        src = source.at[pl.ds(count, count) if to_mate_block else pl.ds(0, count)]
        send = pipe_send.at[2 * n + (1 if to_mate_block else 0)]
        target = {"dp": mate_dp, "pipe": to} if to_mate_block else {"pipe": to}
        return remote(src, target_ref.at[0], send, pipe_recv.at[n], target)

    def loop(lower, upper, body):
        def step(i, carry):
            body(i)
            return carry

        lax.fori_loop(lower, upper, step, 0)

    @pl.when(helper)
    def _():
        to_mate(val).start()
        act_copy(0).start()
        masks[0] = jagged_mask(lb_ref, count).astype(BF)
        masks[1] = jagged_mask(lf_ref, count).astype(BF)
        act_copy(1).start()
        to_mate(que).start()
        to_mate(key).start()
        act_copy(3).start()
        to_mate(gat).start()
        to_mate(out).start()
        act_copy(2).start()

        for i in (out, gat, val, que, key):
            final_copy(i).wait_recv()
            if i == out:
                go_ref[...] = final[i].astype(F32)
            else:
                gp_ref[0, :, home(i)] = final[i].astype(F32)
        for n in range(4):
            act_copy(n).wait_send()
        for i in range(PARTS):
            to_mate(i).wait_send()

    @pl.when(worker)
    def _():
        def send_on(i, chip):
            @pl.when(has_right)
            def _():
                to_right(i, chip).start()

            @pl.when(has_left)
            def _():
                to_left(i, chip).start()

            to_partner(i, chip).start()

        early = 2
        loop(0, early, lambda i: send_on(i, z))

        first, second = slice(0, count), slice(count, 2 * count)

        def prepare(at, tokens):
            normed, inverse = layer_norm(tokens.astype(F32))
            normed_ref[at, :] = normed
            xnb[at, :] = normed.astype(BF)
            norm_t[:, at] = normed.T.astype(BF)
            return inverse

        inverse_own = prepare(first, xb_ref[0])

        def mate_part(i):
            to_left(i, other).wait_recv()
            send_on(i, other)

            @pl.when(i + early < PARTS)
            def _():
                send_on(i + early, z)

        def line(i):
            def tick(t):
                lower, upper = m - t, m + t

                @pl.when(lower >= 0)
                def _():
                    for chip in (2 * lower, 2 * lower + 1):
                        to_right(i, chip).wait_recv()

                        @pl.when(has_right)
                        def _():
                            to_right(i, chip).start()

                        to_partner(i, chip).start()

                @pl.when(upper < pairs)
                def _():
                    for chip in (2 * upper, 2 * upper + 1):
                        to_left(i, chip).wait_recv()

                        @pl.when(has_left)
                        def _():
                            to_left(i, chip).start()

                        to_partner(i, chip).start()

            loop(1, pairs, tick)

        def arrivals(i):
            loop(0, chips, lambda j: from_partner(i, j).wait_recv())

        def project_bwd(i):
            value = dot(xnb[...], wall[i])
            sigma = sigmoid(value)
            silu = value * sigma
            hidden[i] = silu.astype(BF)
            slope[i] = sigma + silu * (1.0 - sigma)

        def project_fwd(i):
            value = dot(xnf[...], wall[i])
            hidden_f[i] = (value * sigmoid(value)).astype(BF)

        mate_part(val)
        g_both[first, :] = g_ref[0]
        g_t[:, first] = g_ref[0].astype(F32).T.astype(BF)
        xnf[first, :] = layer_norm(xf_ref[0].astype(F32))[0].astype(BF)
        act_copy(0).wait_recv()
        inverse_mate = prepare(second, mate_acts[0])
        inverse_b = jnp.concatenate([inverse_own, inverse_mate], axis=0)
        mate_part(que)
        line(val)
        mate_part(key)
        arrivals(val)
        project_bwd(val)
        line(que)
        act_copy(1).wait_recv()
        keeps_b = [jagged_mask(lb_ref, count), mate_masks[0].astype(F32)]
        keeps_f = [jagged_mask(lf_ref, count), mate_masks[1].astype(F32)]
        arrivals(que)
        project_bwd(que)
        act_copy(3).wait_recv()
        xnf[second, :] = layer_norm(mate_acts[2].astype(F32))[0].astype(BF)
        line(key)
        project_fwd(val)
        mate_part(gat)
        arrivals(key)
        project_bwd(key)
        project_fwd(que)
        mate_part(out)

        heads = [slice(head * HEAD_DIM, (head + 1) * HEAD_DIM) for head in range(HEADS)]

        def attend(hidden, keeps):
            sigmas, scores, attns, blocks = [], [], [], []
            for at, keep in zip((first, second), keeps):
                mixed = []
                for cols in heads:
                    score = dot(hidden[que, at, cols], hidden[key, at, cols], NT) * scale
                    sigma = sigmoid(score)
                    attn = (score * sigma * keep).astype(BF)
                    mixed.append(dot(attn, hidden[val, at, cols]))
                    scores.append(score)
                    sigmas.append(sigma)
                    attns.append(attn)
                blocks.append(jnp.concatenate(mixed, axis=1))
            return sigmas, scores, attns, jnp.concatenate(blocks, axis=0)

        def both(pair):
            return pl.ds(2 * pair, 2)

        def part_copy(i, j):
            return remote(
                psend.at[i, both(j)], precv.at[i, both(j)], rs_part.at[i, j], rs_precv.at[i, j], partner
            )

        def right_copy(i, j):
            return remote(
                stage.at[i, both(j)], lrecv.at[i, both(j)], rs_send.at[i, j], rs_lrecv.at[i, j], right
            )

        def left_copy(i, j):
            return remote(
                stage.at[i, both(j)], rrecv.at[i, both(j)], rs_send.at[i, j], rs_rrecv.at[i, j], left
            )

        def terms(i):
            sides, factor = (g_t, gated_b[...]) if i == out else (norm_t, gpre[i])

            def term(k):
                j = jnp.where(2 * m < pairs, pairs - 1 - k, k)
                for d in (2 * j, 2 * j + 1):
                    theirs = dot(sides[rows(d, 1 - c), :], factor) * loss_scale
                    psend[i, d] = theirs.astype(BF)
                part_copy(i, j).start()
                for d in (2 * j, 2 * j + 1):
                    own[i, d] = dot(sides[rows(d, c), :], factor) * loss_scale

            loop(0, pairs, term)

        def chip_sum(i, j):
            part_copy(i, j).wait_recv()
            at = both(j)
            own[i, at] = own[i, at] + precv[i, at].astype(F32)

        def add_left(i, j):
            right_copy(i, j).wait_recv()
            own[i, both(j)] = own[i, both(j)] + lrecv[i, both(j)].astype(F32)

        def add_right(i, j):
            left_copy(i, j).wait_recv()
            own[i, both(j)] = own[i, both(j)] + rrecv[i, both(j)].astype(F32)

        def reduce(i):
            def tick(tau):
                @pl.when(has_right & (tau >= m))
                def _():
                    j = pairs - 1 - tau + m
                    chip_sum(i, j)

                    @pl.when(has_left)
                    def _():
                        add_left(i, j)

                    stage[i, both(j)] = own[i, both(j)].astype(BF)
                    right_copy(i, j).start()

                @pl.when(has_left & (tau >= pairs - 1 - m))
                def _():
                    j = tau - (pairs - 1 - m)
                    chip_sum(i, j)

                    @pl.when(has_right)
                    def _():
                        add_right(i, j)

                    stage[i, both(j)] = own[i, both(j)].astype(BF)
                    left_copy(i, j).start()

            loop(0, pairs - 1, tick)

        def conclude(i):
            chip_sum(i, m)

            @pl.when(has_left)
            def _():
                add_left(i, m)

            @pl.when(has_right)
            def _():
                add_right(i, m)

            stage[i, other] = own[i, other].astype(BF)
            final_copy(i).start()
            if i == out:
                go_ref[...] = own[i, z]
            else:
                gp_ref[0, :, home(i)] = own[i, z]

        line(gat)
        sigmas, scores, attns, mixed = attend(hidden, keeps_b)
        mixed_n, inverse_o = layer_norm(mixed)
        arrivals(gat)
        project_bwd(gat)
        gate = hidden[gat].astype(F32)
        gated_b[...] = (mixed_n * gate).astype(BF)
        act_copy(2).wait_recv()
        g_both[second, :] = mate_acts[1]
        g_t[:, second] = mate_acts[1].astype(F32).T.astype(BF)
        terms(out)
        line(out)
        reduce(out)
        arrivals(out)

        grad_y = dot(g_both[...], wall[out])
        gpre[gat] = (grad_y * mixed_n * slope[gat]).astype(BF)
        terms(gat)
        grad_mixed = norm_back(grad_y * gate, mixed_n, inverse_o).astype(BF)
        reduce(gat)
        blocks = [(b, at, n, cols) for b, at in enumerate((first, second)) for n, cols in enumerate(heads)]
        for b, at, n, cols in blocks:
            grad_vals = dot(attns[b * HEADS + n], grad_mixed[at, cols], TN)
            gpre[val, at, cols] = (grad_vals * slope[val, at, cols]).astype(BF)
        terms(val)
        for b, at, n, cols in blocks:
            score, sigma = scores[b * HEADS + n], sigmas[b * HEADS + n]
            grad_attn = dot(grad_mixed[at, cols], hidden[val, at, cols], NT)
            grad_s = (
                grad_attn * keeps_b[b] * (sigma * (1.0 + score * (1.0 - sigma))) * scale
            ).astype(BF)
            grad_q = dot(grad_s, hidden[key, at, cols])
            grad_k = dot(grad_s, hidden[que, at, cols], TN)
            gpre[que, at, cols] = (grad_q * slope[que, at, cols]).astype(BF)
            gpre[key, at, cols] = (grad_k * slope[key, at, cols]).astype(BF)
        reduce(val)
        terms(que)
        terms(key)
        reduce(que)
        reduce(key)

        row_tile = 256

        def norm_grad(n):
            at = pl.ds(pl.multiple_of(n * row_tile, row_tile), row_tile)
            total = dot(gpre[val], wall[val, at, :], NT)
            for i in (que, key, gat):
                total += dot(gpre[i], wall[i, at, :], NT)
            gnorm[:, at] = total

        loop(0, model // row_tile, norm_grad)
        grad_in = g_both[...].astype(F32) + norm_back(gnorm[...], normed_ref[...], inverse_b)
        bwd_out[...] = grad_in.astype(BF)
        out_copy(1, True).start()
        out_copy(1, False).start()
        conclude(out)

        project_fwd(key)
        project_fwd(gat)
        conclude(gat)
        mixed_f = attend(hidden_f, keeps_f)[3]
        gated_f = (layer_norm(mixed_f)[0] * hidden_f[gat].astype(F32)).astype(BF)
        conclude(val)
        change = dot(gated_f, wall[out], NT)
        fwd_out[second, :] = (mate_acts[2].astype(F32) + change[second]).astype(BF)
        out_copy(0, True).start()
        fwd_out[first, :] = (xf_ref[0].astype(F32) + change[first]).astype(BF)
        out_copy(0, False).start()
        conclude(que)
        conclude(key)

        for n in range(2):
            out_copy(n, True).wait_send()
            out_copy(n, False).wait_send()

        def drain(i):
            final_copy(i).wait_send()

            def each(j):
                to_partner(i, j).wait_send()

                @pl.when(has_right & (lax.div(j, 2) <= m))
                def _():
                    to_right(i, j).wait_send()

                @pl.when(has_left & (lax.div(j, 2) >= m))
                def _():
                    to_left(i, j).wait_send()

            loop(0, chips, each)

            def pair_sends(j):
                part_copy(i, j).wait_send()

                @pl.when(j != m)
                def _():
                    right_copy(i, j).wait_send()

            loop(0, pairs, pair_sends)

        loop(0, PARTS, drain)

    for n in range(2):
        out_copy(n, False).wait_recv()


def finish(*refs):
    sources, targets, held, (ins, outs) = refs[:4], refs[4:8], refs[8:12], refs[12:]
    pieces = []
    for source, target, slot in zip(sources, targets, held):
        step = slot.shape[-2] // 2
        for start in (0, step):
            at = (0,) * (len(slot.shape) - 2) + (pl.ds(start, step),)
            n = len(pieces)
            pieces.append(
                (
                    pltpu.make_async_copy(source.at[at], slot.at[at], ins.at[n]),
                    pltpu.make_async_copy(slot.at[at], target.at[at], outs.at[n]),
                )
            )
    for arrive, _ in pieces:
        arrive.start()
    for arrive, leave in pieces:
        arrive.wait()
        leave.start()
    for _, leave in pieces:
        leave.wait()


def per_device(acts_fwd, acts_bwd, cotangent, lens_fwd, lens_bwd, w_proj, w_out):
    chips = lax.axis_size("dp") // CORES
    phases = lax.axis_size("pipe")
    _, count, model = acts_fwd.shape
    _, shard, proj = w_proj.shape
    hid = w_out.shape[1]
    vmem = pl.BlockSpec(memory_space=pltpu.VMEM)
    hbm = pl.BlockSpec(memory_space=pl.ANY)
    smem = pl.BlockSpec(memory_space=pltpu.SMEM)
    dma = pltpu.SemaphoreType.DMA
    slots = pltpu.VMEM((PARTS, chips, shard, hid), BF)
    flops = 2 * count * model * (2 * proj + 2 * proj + 4 * hid)
    results = (
        jax.ShapeDtypeStruct((1, count, model), BF),
        jax.ShapeDtypeStruct((1, count, model), BF),
        jax.ShapeDtypeStruct((1, shard, proj), F32),
        jax.ShapeDtypeStruct((shard, hid), F32),
    )
    outs = pl.pallas_call(
        functools.partial(kernel, chips, phases),
        out_shape=results,
        in_specs=[vmem, vmem, vmem, smem, smem, vmem, vmem],
        out_specs=(vmem, vmem, vmem, vmem),
        scratch_shapes=[
            pltpu.VMEM((PARTS, model, hid), BF),
            pltpu.VMEM((2 * count, model), BF),
            pltpu.VMEM((2 * count, model), BF),
            pltpu.VMEM((2 * count, model), F32),
            pltpu.VMEM((model, 2 * count), BF),
            pltpu.VMEM((2 * count, model), BF),
            pltpu.VMEM((model, 2 * count), BF),
            pltpu.VMEM((PARTS - 1, 2 * count, hid), BF),
            pltpu.VMEM((PARTS - 1, 2 * count, hid), BF),
            pltpu.VMEM((PARTS - 1, 2 * count, hid), F32),
            pltpu.VMEM((PARTS - 1, 2 * count, hid), BF),
            pltpu.VMEM((2 * count, hid), BF),
            pltpu.VMEM((2 * count, model), F32),
            pltpu.VMEM((2 * count, model), BF),
            pltpu.VMEM((2 * count, model), BF),
            pltpu.VMEM((PARTS, chips, shard, hid), F32),
            slots,
            slots,
            slots,
            slots,
            slots,
            pltpu.VMEM((PARTS, shard, hid), BF),
            pltpu.VMEM((2, count, count), BF),
            pltpu.VMEM((3, count, model), BF),
            pltpu.VMEM((2, count, count), BF),
        ]
        + [dma((PARTS, chips))] * 5
        + [dma((PARTS, chips // 2))] * 5
        + [dma((PARTS,))] * 2
        + [dma((4,))] * 3
        + [dma((2,))],
        compiler_params=pltpu.CompilerParams(
            collective_id=0, has_side_effects=True, vmem_limit_bytes=56 * 1024 * 1024
        ),
        cost_estimate=pl.CostEstimate(
            flops=flops,
            bytes_accessed=4 * shard * (proj + hid),
            transcendentals=2 * count * proj,
        ),
    )(acts_fwd, acts_bwd, cotangent, lens_fwd, lens_bwd, w_proj, w_out[0].T)
    next_acts, prev_grads, grad_proj, grad_out = pl.pallas_call(
        finish,
        out_shape=results,
        in_specs=[hbm] * 4,
        out_specs=(hbm,) * 4,
        scratch_shapes=[pltpu.VMEM(result.shape, result.dtype) for result in results]
        + [dma((8,))] * 2,
    )(*outs)
    return next_acts, prev_grads, grad_proj, grad_out.T[None]


def solution(mesh):
    return jax.shard_map(
        per_device,
        mesh=mesh,
        in_specs=(
            P("pipe", "dp", None),
            P("pipe", "dp", None),
            P("pipe", "dp", None),
            P("pipe", "dp", None),
            P("pipe", "dp", None),
            P("pipe", "dp", None),
            P("pipe", None, "dp"),
        ),
        out_specs=(
            P("pipe", "dp", None),
            P("pipe", "dp", None),
            P("pipe", "dp", None),
            P("pipe", None, "dp"),
        ),
        check_vma=False,
    )
```

```python
import functools
import math

import jax
import jax.numpy as jnp
from jax import lax
from jax.experimental import pallas as pl
from jax.experimental.pallas import tpu as pltpu
from jax.sharding import PartitionSpec as P

HEADS = 4
HEAD_DIM = 128
LMAX = 64
EPS = 1e-05
CORES = 2
PARTS = 5
MESH = pl.DeviceIdType.MESH
BF = jnp.bfloat16
F32 = jnp.float32

NN = (((1,), (0,)), ((), ()))
NT = (((1,), (1,)), ((), ()))
TN = (((0,), (0,)), ((), ()))


def dot(a, b, dims=NN):
    return lax.dot_general(a, b, dims, preferred_element_type=F32)


def sigmoid(v):
    return 0.5 + 0.5 * jnp.tanh(0.5 * v)


def layer_norm(values):
    center = values - jnp.mean(values, axis=-1, keepdims=True)
    inverse = lax.rsqrt(jnp.mean(center * center, axis=-1, keepdims=True) + EPS)
    return center * inverse, inverse


def norm_back(grad, normed, inverse):
    return inverse * (
        grad
        - jnp.mean(grad, axis=-1, keepdims=True)
        - normed * jnp.mean(grad * normed, axis=-1, keepdims=True)
    )


def jagged_mask(lens_ref, count):
    rows = lax.broadcasted_iota(jnp.int32, (count, count), 0)
    cols = lax.broadcasted_iota(jnp.int32, (count, count), 1)
    row_seg = jnp.zeros((count, count), jnp.int32)
    col_seg = jnp.zeros((count, count), jnp.int32)
    end = jnp.int32(0)
    for user in range(lens_ref.shape[2]):
        end = end + lens_ref[0, 0, user]
        row_seg += jnp.where(rows >= end, 1, 0)
        col_seg += jnp.where(cols >= end, 1, 0)
    keep = (row_seg == col_seg) & (cols <= rows)
    return jnp.where(keep, 1.0 / LMAX, 0.0)


def kernel(
    chips,
    phases,
    xf_ref,
    xb_ref,
    g_ref,
    lf_ref,
    lb_ref,
    wp_ref,
    wo_ref,
    next_ref,
    prev_ref,
    gp_ref,
    go_ref,
    wall,
    xnf,
    xnb,
    normed_ref,
    norm_t,
    norm_s,
    g_both,
    g_t,
    g_s,
    hidden,
    hidden_f,
    slope,
    gpre,
    gated_b,
    gnorm,
    fwd_out,
    bwd_out,
    own,
    psend,
    precv,
    lrecv,
    rrecv,
    stage,
    final,
    masks,
    mate_acts,
    mate_masks,
    ag_right,
    ag_left,
    ag_part,
    ag_chain,
    ag_precv,
    rs_send,
    rs_part,
    rs_precv,
    rs_lrecv,
    rs_rrecv,
    fin_send,
    fin_recv,
    act_send,
    act_recv,
    pipe_send,
    pipe_recv,
):
    val, que, key, gat, out = range(PARTS)
    shard, hid = wo_ref.shape
    count, model = xf_ref.shape[1:]
    scale = HEAD_DIM ** (-0.5)
    loss_scale = 1.0 / math.sqrt(chips * CORES * count)
    me = lax.axis_index("dp")
    phase = lax.axis_index("pipe")
    z, c = lax.div(me, CORES), lax.rem(me, CORES)

    pairs = chips // 2
    m = lax.div(z, 2)

    def inner(pair):
        return 2 * pair + jnp.where(2 * pair < pairs, 1, 0)

    worker = z == inner(m)
    helper = jnp.logical_not(worker)
    other = 4 * m + 1 - z
    has_left, has_right = m > 0, m < pairs - 1
    mate_dp = other * CORES + c
    mate, partner = {"dp": mate_dp}, {"dp": z * CORES + 1 - c}
    left, right = {"dp": inner(m - 1) * CORES + c}, {"dp": inner(m + 1) * CORES + c}
    ahead = lax.rem(phase + 1, phases)
    behind = lax.rem(phase + phases - 1, phases)

    barrier = pltpu.get_barrier_semaphore()

    def greet(target):
        pl.semaphore_signal(barrier, inc=1, device_id=target, device_id_type=MESH)

    greet(mate)

    @pl.when(helper)
    def _():
        greet({"dp": mate_dp, "pipe": ahead})
        greet({"dp": mate_dp, "pipe": behind})

    @pl.when(worker)
    def _():
        greet(partner)
        greet({"pipe": ahead})
        greet({"pipe": behind})

        @pl.when(has_left)
        def _():
            greet(left)

        @pl.when(has_right)
        def _():
            greet(right)

    def rows(chip, core):
        return pl.ds(pl.multiple_of((chip * CORES + core) * shard, shard), shard)

    def home(i):
        start = (i + 1) % (PARTS - 1) * hid
        return slice(start, start + hid)

    for i in (val, que, key, gat):
        wall[i, rows(z, c), :] = wp_ref[0, :, home(i)].astype(BF)
    wall[out, rows(z, c), :] = wo_ref[...].astype(BF)

    peers = jnp.where(worker, 6 + jnp.where(has_left, 1, 0) + jnp.where(has_right, 1, 0), 1)
    pl.semaphore_wait(barrier, peers)

    def remote(src, dst, send_sem, recv_sem, target):
        return pltpu.make_async_remote_copy(
            src_ref=src,
            dst_ref=dst,
            send_sem=send_sem,
            recv_sem=recv_sem,
            device_id=target,
            device_id_type=MESH,
        )

    def gather(i, chip, core, send_sem, recv_sem, target):
        block = wall.at[i, rows(chip, core), :]
        return remote(block, block, send_sem.at[i, chip], recv_sem.at[i, chip], target)

    def to_right(i, chip):
        return gather(i, chip, c, ag_right, ag_chain, right)

    def to_left(i, chip):
        return gather(i, chip, c, ag_left, ag_chain, left)

    def to_mate(i):
        return gather(i, z, c, ag_right, ag_chain, mate)

    def to_partner(i, chip):
        return gather(i, chip, c, ag_part, ag_precv, partner)

    def from_partner(i, chip):
        return gather(i, chip, 1 - c, ag_part, ag_precv, partner)

    def act_copy(n):
        src, dst = (
            (xb_ref.at[0], mate_acts.at[0]),
            (masks, mate_masks),
            (g_ref.at[0], mate_acts.at[1]),
            (xf_ref.at[0], mate_acts.at[2]),
        )[n]
        return remote(src, dst, act_send.at[n], act_recv.at[n], mate)

    def final_copy(i):
        return remote(stage.at[i, other], final.at[i], fin_send.at[i], fin_recv.at[i], mate)

    def out_copy(n, to_mate_block):
        source, target_ref, to = ((fwd_out, next_ref, ahead), (bwd_out, prev_ref, behind))[n]
        src = source.at[pl.ds(count, count) if to_mate_block else pl.ds(0, count)]
        send = pipe_send.at[2 * n + (1 if to_mate_block else 0)]
        target = {"dp": mate_dp, "pipe": to} if to_mate_block else {"pipe": to}
        return remote(src, target_ref.at[0], send, pipe_recv.at[n], target)

    def loop(lower, upper, body):
        def step(i, carry):
            body(i)
            return carry

        lax.fori_loop(lower, upper, step, 0)

    @pl.when(helper)
    def _():
        to_mate(val).start()
        act_copy(0).start()
        masks[0] = jagged_mask(lb_ref, count).astype(BF)
        masks[1] = jagged_mask(lf_ref, count).astype(BF)
        act_copy(1).start()
        to_mate(que).start()
        to_mate(key).start()
        to_mate(gat).start()
        to_mate(out).start()
        act_copy(2).start()
        act_copy(3).start()

        for i in (out, gat, val, que, key):
            final_copy(i).wait_recv()
            if i == out:
                go_ref[...] = final[i].astype(F32)
            else:
                gp_ref[0, :, home(i)] = final[i].astype(F32)
        for n in range(4):
            act_copy(n).wait_send()
        for i in range(PARTS):
            to_mate(i).wait_send()

    @pl.when(worker)
    def _():
        def send_on(i, chip):
            @pl.when(has_right)
            def _():
                to_right(i, chip).start()

            @pl.when(has_left)
            def _():
                to_left(i, chip).start()

            to_partner(i, chip).start()

        early = 2
        loop(0, early, lambda i: send_on(i, z))

        first, second = slice(0, count), slice(count, 2 * count)

        def prepare(at, tokens):
            normed, inverse = layer_norm(tokens.astype(F32))
            normed_ref[at, :] = normed
            xnb[at, :] = normed.astype(BF)
            norm_t[:, at] = normed.T.astype(BF)
            return inverse

        inverse_own = prepare(first, xb_ref[0])

        def mate_part(i):
            to_left(i, other).wait_recv()
            send_on(i, other)

            @pl.when(i + early < PARTS)
            def _():
                send_on(i + early, z)

        def line(i):
            def tick(t):
                lower, upper = m - t, m + t

                @pl.when(lower >= 0)
                def _():
                    for chip in (2 * lower, 2 * lower + 1):
                        to_right(i, chip).wait_recv()

                        @pl.when(has_right)
                        def _():
                            to_right(i, chip).start()

                        to_partner(i, chip).start()

                @pl.when(upper < pairs)
                def _():
                    for chip in (2 * upper, 2 * upper + 1):
                        to_left(i, chip).wait_recv()

                        @pl.when(has_left)
                        def _():
                            to_left(i, chip).start()

                        to_partner(i, chip).start()

            loop(1, pairs, tick)

        def arrivals(i):
            loop(0, chips, lambda j: from_partner(i, j).wait_recv())

        def project_bwd(i):
            value = dot(xnb[...], wall[i])
            sigma = sigmoid(value)
            silu = value * sigma
            hidden[i] = silu.astype(BF)
            slope[i] = sigma + silu * (1.0 - sigma)

        def project_fwd(i):
            value = dot(xnf[...], wall[i])
            hidden_f[i] = (value * sigmoid(value)).astype(BF)

        def sort_rows(by_row, sorted_ref):
            for d in range(chips):
                at = pl.ds(d * shard, shard)
                sorted_ref[0, at, :] = by_row[rows(d, c), :]
                sorted_ref[1, at, :] = by_row[rows(d, 1 - c), :]

        mate_part(val)
        g_both[first, :] = g_ref[0]
        g_t[:, first] = g_ref[0].astype(F32).T.astype(BF)
        xnf[first, :] = layer_norm(xf_ref[0].astype(F32))[0].astype(BF)
        act_copy(0).wait_recv()
        inverse_mate = prepare(second, mate_acts[0])
        inverse_b = jnp.concatenate([inverse_own, inverse_mate], axis=0)
        mate_part(que)
        line(val)
        mate_part(key)
        arrivals(val)
        project_bwd(val)
        line(que)
        act_copy(1).wait_recv()
        keeps_b = [jagged_mask(lb_ref, count), mate_masks[0].astype(F32)]
        keeps_f = [jagged_mask(lf_ref, count), mate_masks[1].astype(F32)]
        arrivals(que)
        project_bwd(que)
        mate_part(gat)
        line(key)
        sort_rows(norm_t, norm_s)
        mate_part(out)
        arrivals(key)
        project_bwd(key)

        heads = [slice(head * HEAD_DIM, (head + 1) * HEAD_DIM) for head in range(HEADS)]

        def attend(hidden, keeps):
            sigmas, scores, attns, blocks = [], [], [], []
            for at, keep in zip((first, second), keeps):
                mixed = []
                for cols in heads:
                    score = dot(hidden[que, at, cols], hidden[key, at, cols], NT) * scale
                    sigma = sigmoid(score)
                    attn = (score * sigma * keep).astype(BF)
                    mixed.append(dot(attn, hidden[val, at, cols]))
                    scores.append(score)
                    sigmas.append(sigma)
                    attns.append(attn)
                blocks.append(jnp.concatenate(mixed, axis=1))
            return sigmas, scores, attns, jnp.concatenate(blocks, axis=0)

        def both(pair):
            return pl.ds(2 * pair, 2)

        def part_copy(i, j):
            return remote(
                psend.at[i, both(j)], precv.at[i, both(j)], rs_part.at[i, j], rs_precv.at[i, j], partner
            )

        def right_copy(i, d):
            return remote(
                stage.at[i, d], lrecv.at[i, d], rs_send.at[i, d], rs_lrecv.at[i, d], right
            )

        def left_copy(i, d):
            return remote(
                stage.at[i, d], rrecv.at[i, d], rs_send.at[i, d], rs_rrecv.at[i, d], left
            )

        def outer_first(j):
            return (4 * j + 1 - inner(j), inner(j))

        def terms(i):
            sides, factor = (g_s, gated_b[...]) if i == out else (norm_s, gpre[i])
            whole = (chips, shard, hid)
            psend[i] = (dot(sides[1], factor) * loss_scale).astype(BF).reshape(whole)

            def pass_pair(k):
                part_copy(i, jnp.where(2 * m < pairs, pairs - 1 - k, k)).start()

            loop(0, pairs, pass_pair)
            own[i] = (dot(sides[0], factor) * loss_scale).reshape(whole)

        def chip_sum(i, j):
            part_copy(i, j).wait_recv()

        def summed(i, d, from_left, from_right):
            own[i, d] = own[i, d] + precv[i, d].astype(F32)

            @pl.when(from_left)
            def _():
                right_copy(i, d).wait_recv()
                own[i, d] = own[i, d] + lrecv[i, d].astype(F32)

            @pl.when(from_right)
            def _():
                left_copy(i, d).wait_recv()
                own[i, d] = own[i, d] + rrecv[i, d].astype(F32)

        def reduce(i):
            def tick(tau):
                @pl.when(has_right & (tau >= m))
                def _():
                    j = pairs - 1 - tau + m
                    chip_sum(i, j)
                    for d in outer_first(j):
                        summed(i, d, has_left, False)
                        stage[i, d] = own[i, d].astype(BF)
                        right_copy(i, d).start()

                @pl.when(has_left & (tau >= pairs - 1 - m))
                def _():
                    j = tau - (pairs - 1 - m)
                    chip_sum(i, j)
                    for d in outer_first(j):
                        summed(i, d, False, has_right)
                        stage[i, d] = own[i, d].astype(BF)
                        left_copy(i, d).start()

            loop(0, pairs - 1, tick)

        def conclude(i):
            chip_sum(i, m)
            summed(i, other, has_left, has_right)
            stage[i, other] = own[i, other].astype(BF)
            final_copy(i).start()
            summed(i, z, has_left, has_right)
            if i == out:
                go_ref[...] = own[i, z]
            else:
                gp_ref[0, :, home(i)] = own[i, z]

        line(gat)
        sigmas, scores, attns, mixed = attend(hidden, keeps_b)
        mixed_n, inverse_o = layer_norm(mixed)
        arrivals(gat)
        project_bwd(gat)
        gate = hidden[gat].astype(F32)
        gated_b[...] = (mixed_n * gate).astype(BF)
        act_copy(2).wait_recv()
        g_both[second, :] = mate_acts[1]
        g_t[:, second] = mate_acts[1].astype(F32).T.astype(BF)
        sort_rows(g_t, g_s)
        terms(out)
        line(out)
        reduce(out)
        arrivals(out)

        grad_y = dot(g_both[...], wall[out])
        gpre[gat] = (grad_y * mixed_n * slope[gat]).astype(BF)
        terms(gat)
        grad_mixed = norm_back(grad_y * gate, mixed_n, inverse_o).astype(BF)
        reduce(gat)
        blocks = [(b, at, n, cols) for b, at in enumerate((first, second)) for n, cols in enumerate(heads)]
        for b, at, n, cols in blocks:
            grad_vals = dot(attns[b * HEADS + n], grad_mixed[at, cols], TN)
            gpre[val, at, cols] = (grad_vals * slope[val, at, cols]).astype(BF)
        terms(val)
        for b, at, n, cols in blocks:
            score, sigma = scores[b * HEADS + n], sigmas[b * HEADS + n]
            grad_attn = dot(grad_mixed[at, cols], hidden[val, at, cols], NT)
            grad_s = (
                grad_attn * keeps_b[b] * (sigma * (1.0 + score * (1.0 - sigma))) * scale
            ).astype(BF)
            grad_q = dot(grad_s, hidden[key, at, cols])
            grad_k = dot(grad_s, hidden[que, at, cols], TN)
            gpre[que, at, cols] = (grad_q * slope[que, at, cols]).astype(BF)
            gpre[key, at, cols] = (grad_k * slope[key, at, cols]).astype(BF)
        reduce(val)
        terms(que)
        terms(key)
        reduce(que)
        reduce(key)

        row_tile = 256

        def norm_grad(n):
            at = pl.ds(pl.multiple_of(n * row_tile, row_tile), row_tile)
            total = dot(gpre[val], wall[val, at, :], NT)
            for i in (que, key, gat):
                total += dot(gpre[i], wall[i, at, :], NT)
            gnorm[:, at] = total

        loop(0, model // row_tile, norm_grad)
        grad_in = g_both[...].astype(F32) + norm_back(gnorm[...], normed_ref[...], inverse_b)
        bwd_out[...] = grad_in.astype(BF)
        out_copy(1, True).start()
        out_copy(1, False).start()
        conclude(out)

        act_copy(3).wait_recv()
        xnf[second, :] = layer_norm(mate_acts[2].astype(F32))[0].astype(BF)
        loop(0, PARTS - 1, project_fwd)
        conclude(gat)
        mixed_f = attend(hidden_f, keeps_f)[3]
        gated_f = (layer_norm(mixed_f)[0] * hidden_f[gat].astype(F32)).astype(BF)
        conclude(val)
        change = dot(gated_f, wall[out], NT)
        fwd_out[second, :] = (mate_acts[2].astype(F32) + change[second]).astype(BF)
        out_copy(0, True).start()
        fwd_out[first, :] = (xf_ref[0].astype(F32) + change[first]).astype(BF)
        out_copy(0, False).start()
        conclude(que)
        conclude(key)

        for n in range(2):
            out_copy(n, True).wait_send()
            out_copy(n, False).wait_send()

        def drain(i):
            final_copy(i).wait_send()

            def each(j):
                to_partner(i, j).wait_send()

                @pl.when(has_right & (lax.div(j, 2) <= m))
                def _():
                    to_right(i, j).wait_send()

                @pl.when(has_left & (lax.div(j, 2) >= m))
                def _():
                    to_left(i, j).wait_send()

            loop(0, chips, each)

            def pair_sends(j):
                part_copy(i, j).wait_send()

                @pl.when(j != m)
                def _():
                    right_copy(i, 2 * j).wait_send()
                    right_copy(i, 2 * j + 1).wait_send()

            loop(0, pairs, pair_sends)

        loop(0, PARTS, drain)

    for n in range(2):
        out_copy(n, False).wait_recv()


def finish(*refs):
    sources, targets, held, (ins, outs) = refs[:4], refs[4:8], refs[8:12], refs[12:]
    pieces = []
    for source, target, slot in zip(sources, targets, held):
        step = slot.shape[-2] // 2
        for start in (0, step):
            at = (0,) * (len(slot.shape) - 2) + (pl.ds(start, step),)
            n = len(pieces)
            pieces.append(
                (
                    pltpu.make_async_copy(source.at[at], slot.at[at], ins.at[n]),
                    pltpu.make_async_copy(slot.at[at], target.at[at], outs.at[n]),
                )
            )
    for arrive, _ in pieces:
        arrive.start()
    for arrive, leave in pieces:
        arrive.wait()
        leave.start()
    for _, leave in pieces:
        leave.wait()


def per_device(acts_fwd, acts_bwd, cotangent, lens_fwd, lens_bwd, w_proj, w_out):
    chips = lax.axis_size("dp") // CORES
    phases = lax.axis_size("pipe")
    _, count, model = acts_fwd.shape
    _, shard, proj = w_proj.shape
    hid = w_out.shape[1]
    vmem = pl.BlockSpec(memory_space=pltpu.VMEM)
    hbm = pl.BlockSpec(memory_space=pl.ANY)
    smem = pl.BlockSpec(memory_space=pltpu.SMEM)
    dma = pltpu.SemaphoreType.DMA
    slots = pltpu.VMEM((PARTS, chips, shard, hid), BF)
    flops = 2 * count * model * (2 * proj + 2 * proj + 4 * hid)
    results = (
        jax.ShapeDtypeStruct((1, count, model), BF),
        jax.ShapeDtypeStruct((1, count, model), BF),
        jax.ShapeDtypeStruct((1, shard, proj), F32),
        jax.ShapeDtypeStruct((shard, hid), F32),
    )
    outs = pl.pallas_call(
        functools.partial(kernel, chips, phases),
        out_shape=results,
        in_specs=[vmem, vmem, vmem, smem, smem, vmem, vmem],
        out_specs=(vmem, vmem, vmem, vmem),
        scratch_shapes=[
            pltpu.VMEM((PARTS, model, hid), BF),
            pltpu.VMEM((2 * count, model), BF),
            pltpu.VMEM((2 * count, model), BF),
            pltpu.VMEM((2 * count, model), F32),
            pltpu.VMEM((model, 2 * count), BF),
            pltpu.VMEM((2, model // 2, 2 * count), BF),
            pltpu.VMEM((2 * count, model), BF),
            pltpu.VMEM((model, 2 * count), BF),
            pltpu.VMEM((2, model // 2, 2 * count), BF),
            pltpu.VMEM((PARTS - 1, 2 * count, hid), BF),
            pltpu.VMEM((PARTS - 1, 2 * count, hid), BF),
            pltpu.VMEM((PARTS - 1, 2 * count, hid), F32),
            pltpu.VMEM((PARTS - 1, 2 * count, hid), BF),
            pltpu.VMEM((2 * count, hid), BF),
            pltpu.VMEM((2 * count, model), F32),
            pltpu.VMEM((2 * count, model), BF),
            pltpu.VMEM((2 * count, model), BF),
            pltpu.VMEM((PARTS, chips, shard, hid), F32),
            slots,
            slots,
            slots,
            slots,
            slots,
            pltpu.VMEM((PARTS, shard, hid), BF),
            pltpu.VMEM((2, count, count), BF),
            pltpu.VMEM((3, count, model), BF),
            pltpu.VMEM((2, count, count), BF),
        ]
        + [dma((PARTS, chips))] * 10
        + [dma((PARTS,))] * 2
        + [dma((4,))] * 3
        + [dma((2,))],
        compiler_params=pltpu.CompilerParams(
            collective_id=0, has_side_effects=True, vmem_limit_bytes=56 * 1024 * 1024
        ),
        cost_estimate=pl.CostEstimate(
            flops=flops,
            bytes_accessed=4 * shard * (proj + hid),
            transcendentals=2 * count * proj,
        ),
    )(acts_fwd, acts_bwd, cotangent, lens_fwd, lens_bwd, w_proj, w_out[0].T)
    next_acts, prev_grads, grad_proj, grad_out = pl.pallas_call(
        finish,
        out_shape=results,
        in_specs=[hbm] * 4,
        out_specs=(hbm,) * 4,
        scratch_shapes=[pltpu.VMEM(result.shape, result.dtype) for result in results]
        + [dma((8,))] * 2,
    )(*outs)
    return next_acts, prev_grads, grad_proj, grad_out.T[None]


def solution(mesh):
    return jax.shard_map(
        per_device,
        mesh=mesh,
        in_specs=(
            P("pipe", "dp", None),
            P("pipe", "dp", None),
            P("pipe", "dp", None),
            P("pipe", "dp", None),
            P("pipe", "dp", None),
            P("pipe", "dp", None),
            P("pipe", None, "dp"),
        ),
        out_specs=(
            P("pipe", "dp", None),
            P("pipe", "dp", None),
            P("pipe", "dp", None),
            P("pipe", None, "dp"),
        ),
        check_vma=False,
    )
```
